256 devices in a mesh: dp: 16 (over x, y), ep: 8 (over z), tp: 2 (over core).
Axes of the slice: x: 4, y: 4, z: 8, core: 2. Of those that a mesh axis runs over, the one named last changes fastest.
Arguments:
- queries: bfloat16 [2048, 64, 576], P('dp', ('ep', 'tp')), may hold values from -18 to 18
- cache: bfloat16 [64, 256, 576], P('dp'), may hold values from -4 to 4
- span_latent: bfloat16 [64, 32, 576], P('dp'), may hold values from -4 to 4
- prefix_len: int32 [64], replicated, may hold values from 1 to 256, as said below
- destination: int32 [2, 16], replicated, may hold values from 0 to 15, each once within a row
- uv_weight: bfloat16 [64, 512, 128], P(('ep', 'tp')), may hold values from -0.25 to 0.25
- out_weight: bfloat16 [8192, 7168], P(('ep', 'tp'), 'dp'), may hold values from -0.0625 to 0.0625
- residual: bfloat16 [2048, 7168], P('dp'), may hold values from -6 to 6
- norm_gain: bfloat16 [7168], replicated, may hold values from 0.25 to 1.75
- routes: int32 [2048, 2], P('dp'), may hold values from 0 to 15, all different within a row; in each aligned block of 128 rows (0 to 127, 128 to 255, ...) at most 24 rows name the same one
- route_weight: bfloat16 [2048, 2], P('dp'), may hold values from 0.19921875 to 1
- gate_weight: bfloat16 [16, 7168, 2048], P('dp', None, ('ep', 'tp')), may hold values from -0.0625 to 0.0625
- up_weight: bfloat16 [16, 7168, 2048], P('dp', None, ('ep', 'tp')), may hold values from -0.0625 to 0.0625
- down_weight: bfloat16 [16, 2048, 7168], P('dp', ('ep', 'tp')), may hold values from -0.125 to 0.125
Outputs:
- output: bfloat16 [2048, 7168], P(('dp', 'ep', 'tp'))
The draws below stay inside these ranges and needn't reach their ends.
Inputs may be any that keep to these rules, and one draw needn't show every extreme that they name: `prefix_len`: some request holds exactly 256 rows. `destination`: each row is a permutation of the ranks. `routes`: each row names 2 different experts; within the tokens of one rank no expert is named more than 24 times, a bound that some block reaches.
All inputs are finite; a program needn't handle non-finite values.
Results may differ from the reference program's by a relative error of at most 0.02.
Values may be sent and summed in bfloat16 or wider, within the bound.
No kernel may reach another device: no remote copies, remote signals or barrier semaphores. Data moves between devices by JAX's collectives and lax.ppermute only.
A program may use at most 128 MiB of HBM per device.

```python
import math
from functools import partial
import jax
import jax.numpy as jnp
import numpy as np
from jax import lax

D = 7168
LAT = 512
VH = 128
FFE = 2048
TOPK = 2
REQ = 4
PRE = 256
CHK = 32
CW = 576
HEADS = 64
FF_DEV = 128
EXPERTS = 16
TOK = 128
CAPR = 24
N_DP = 16
N_EP = 8
N_TP = 2


def draw_cache(key, part):
    key = jax.random.fold_in(key, 11)
    base = jnp.clip(jax.random.normal(key, (N_DP * REQ, PRE, CW), jnp.float32), -4.0, 4.0)
    return base.astype(jnp.bfloat16)


def draw_span_latent(key, part):
    key = jax.random.fold_in(key, 23)
    base = jnp.clip(jax.random.normal(key, (N_DP * REQ, CHK, CW), jnp.float32), -4.0, 4.0)
    return base.astype(jnp.bfloat16)


def draw_queries(key, part):
    key = jax.random.fold_in(key, 37)
    base = jnp.clip(jax.random.normal(key, (N_DP * TOK, HEADS, CW), jnp.float32), -4.0, 4.0)
    return base.astype(jnp.bfloat16)


def draw_prefix_len(key, part):
    key = jax.random.fold_in(key, 41)
    first_key, second_key = jax.random.split(key)
    counts = jax.random.randint(first_key, (N_DP * REQ,), 1, PRE + 1)
    chosen = jax.random.randint(second_key, (), 0, N_DP * REQ)
    return counts.at[chosen].set(PRE).astype(jnp.int32)


def level_of(own_key, dims, cuts, smallest, top_value):
    def one(dim, shards_of):
        steps = jax.random.uniform(jax.random.fold_in(jax.random.fold_in(own_key, 6), dim), (shards_of,), jnp.float32, smallest / len(cuts), top_value / len(cuts))
        return jnp.repeat(jnp.exp(steps), dims[dim] // shards_of).reshape((-1,) + (1,) * (len(dims) - dim - 1))

    level = one(*cuts[0])
    for cut in cuts[1:]:
        level = level * one(*cut)
    return level


def assign_block(key, own, number, rows, amount, top, most, lean):
    order = jax.random.permutation(key, amount)
    packed, common = portions_of(amount, rows * top, most, lean, True), portions_of(amount, rows * top, most, lean, False)
    places = jnp.arange(amount)

    def named(sizes, rotation):
        used = int((sizes > 0).sum())
        fixed = max(1, used // 4)
        shifted = fixed + (places - fixed + rotation * (used - fixed)) % max(1, amount - fixed)
        return jnp.zeros((amount,), jnp.int32).at[order[jnp.where(places < fixed, places, shifted)]].set(jnp.asarray(sizes, jnp.int32))

    sizes = jnp.where(number % 4 == 0, named(packed, number // 4), named(common, number - number // 4 - 1))
    mixed = jax.random.permutation(jax.random.fold_in(own, 3), amount)
    source_of, receiver = mixed[0:amount // 2 * 2:2], mixed[1:amount // 2 * 2:2]
    slack = jnp.minimum(sizes[source_of] - 1, most - sizes[receiver]) // 2
    slack = jnp.where((source_of == order[0]) | (receiver == order[0]) | (sizes[receiver] == 0), 0, jnp.maximum(slack, 0))
    shifted = jax.random.randint(jax.random.fold_in(own, 4), (amount // 2,), 0, 1 << 20) % (slack + 1)
    sizes = sizes.at[source_of].add(-shifted).at[receiver].add(shifted)
    labels = jnp.searchsorted(jnp.cumsum(sizes), jnp.arange(rows * top), side="right").astype(jnp.int32)
    listing = labels.reshape(top, rows).T
    listing = listing[jax.random.permutation(jax.random.fold_in(own, 1), rows)]
    rotation = jax.random.randint(jax.random.fold_in(own, 2), (rows, 1), 0, top)
    return jnp.take_along_axis(listing, (jnp.arange(top)[None, :] + rotation) % top, axis=1)


def portions_of(count, total, bound, skew, full):
    portions = [(1 << 20) // math.isqrt(standing ** skew) + 1 for standing in range(1, count + 1)]
    largest = bound if full else min(bound, max(-(-total // count), total * portions[0] // sum(portions)))
    least = 1 if total - largest >= count - 1 else 0
    given, surplus = [largest] + [least] * (count - 1), total - largest - least * (count - 1)
    while surplus > 0:
        free = [i for i in range(1, count) if given[i] < largest] or [i for i in range(1, count) if given[i] < bound]
        whole, remaining = sum([portions[i] for i in free]), surplus
        for i in free:
            addition = min(bound - given[i], max(1, remaining * portions[i] // whole), surplus)
            given[i] = given[i] + addition
            surplus = surplus - addition
    return np.array(given)


def scatter_about(own_key, dims, deviation, limit, shards=(), kind=jnp.bfloat16):
    array = jax.random.normal(own_key, dims, jnp.float32) * deviation
    if len(shards) > 0:
        array = level_of(own_key, dims, shards, -0.22, 0.18) * array
    return jnp.clip(array, min=-limit, max=limit).astype(kind)


def setup_inputs(seed: int = 0) -> dict:
    arg_keys = jax.random.split(jax.random.key(seed), 15)
    queries = draw_queries(jax.random.fold_in(arg_keys[14], 71), 0)
    cache = draw_cache(jax.random.fold_in(arg_keys[14], 71), 0)
    span_latent = draw_span_latent(jax.random.fold_in(arg_keys[14], 71), 0)
    prefix_len = draw_prefix_len(jax.random.fold_in(arg_keys[14], 71), 0)
    destination = jax.vmap(lambda own: jax.random.permutation(own, N_DP))(jax.random.split(arg_keys[4], 2)).reshape((2, N_DP)).astype(jnp.int32)
    uv_weight = scatter_about(arg_keys[5], (HEADS, LAT, VH), LAT ** -0.5, 0.25, ((0, 16),))
    out_weight = scatter_about(arg_keys[6], (HEADS * VH, D), (HEADS * VH) ** -0.5, 0.0625, ((0, 16), (1, 16)))
    residual = scatter_about(arg_keys[7], (N_DP * TOK, D), 1.0, 6.0, ((0, 16),))
    norm_gain = jnp.clip(1.0 + 0.15 * jax.random.normal(arg_keys[8], (D,), jnp.float32), 0.25, 1.75).astype(jnp.bfloat16)
    routes_keys = jax.random.split(jax.random.fold_in(arg_keys[9], 1), (N_DP * TOK) // TOK)
    routes_turns = jax.random.permutation(jax.random.fold_in(arg_keys[9], 3), (N_DP * TOK) // TOK)
    routes = jax.vmap(lambda own, number: assign_block(jax.random.fold_in(arg_keys[9], 2), own, number, TOK, EXPERTS, TOPK, CAPR, 2))(routes_keys, routes_turns).reshape((N_DP * TOK, TOPK))
    route_weight = jnp.clip(0.19921875 + 0.80078125 * jax.random.uniform(arg_keys[10], (N_DP * TOK, TOPK), jnp.float32) ** level_of(arg_keys[10], (N_DP * TOK, TOPK), ((0, 16),), -0.2, 0.2), 0.19921875, 1.0).astype(jnp.bfloat16)
    gate_weight = scatter_about(arg_keys[11], (EXPERTS, D, FFE), D ** -0.5, 0.0625, ((0, 16), (2, 16)))
    up_weight = scatter_about(arg_keys[12], (EXPERTS, D, FFE), D ** -0.5, 0.0625, ((0, 16), (2, 16)))
    down_weight = scatter_about(arg_keys[13], (EXPERTS, FFE, D), FFE ** -0.5, 0.125, ((0, 16), (1, 16)))
    return {"queries": queries, "cache": cache, "span_latent": span_latent, "prefix_len": prefix_len, "destination": destination, "uv_weight": uv_weight, "out_weight": out_weight, "residual": residual, "norm_gain": norm_gain, "routes": routes, "route_weight": route_weight, "gate_weight": gate_weight, "up_weight": up_weight, "down_weight": down_weight}


score_scale = 192.0 ** (-0.5)
norm_eps = 1e-06

def key_mask(lengths, prefix_rows, span_rows):
    key_index = jnp.arange(prefix_rows + span_rows, dtype=jnp.int32)
    query_index = jnp.arange(span_rows, dtype=jnp.int32)
    in_prefix = (key_index < prefix_rows) & (key_index < lengths[..., None])
    in_span = (key_index[None, :] >= prefix_rows) & (key_index[None, :] - prefix_rows <= query_index[:, None])
    return in_prefix[..., None, :] | in_span

def rms_norm(rows, gain):
    widened = rows.astype(jnp.float32)
    factor = lax.rsqrt(lax.optimization_barrier(jnp.mean(widened * widened, axis=-1, keepdims=True)) + norm_eps)
    return (widened * factor * gain.astype(jnp.float32)).astype(jnp.bfloat16)

def slot_tables(route_rows, weight_rows, experts, capacity):
    top_k = route_rows.shape[1]
    flat_routes = route_rows.reshape(-1).astype(jnp.int32)
    hits = (flat_routes[:, None] == jnp.arange(experts, dtype=jnp.int32)[None, :]).astype(jnp.int32)
    earlier = jnp.cumsum(hits, axis=0) - hits
    position = lax.optimization_barrier(jnp.sum(earlier * hits, axis=1))
    slot_of = flat_routes * capacity + position
    matches = jnp.arange(experts * capacity, dtype=jnp.int32)[:, None] == slot_of[None, :]
    matches = matches.reshape(experts * capacity, route_rows.shape[0], top_k)
    placer = jnp.any(matches, axis=-1).astype(jnp.bfloat16)
    combiner = lax.optimization_barrier(jnp.sum(jnp.where(matches, weight_rows[None], jnp.zeros((), weight_rows.dtype)), axis=-1)).T
    return (placer, combiner)

def reference(queries, cache, span_latent, prefix_len, destination, uv_weight, out_weight, residual, norm_gain, routes, route_weight, gate_weight, up_weight, down_weight):
    rank_count = N_DP
    members = N_EP * N_TP
    ranks = jnp.arange(rank_count, dtype=jnp.int32)
    source_first = jnp.zeros((rank_count,), jnp.int32).at[destination[0]].set(ranks)
    source_second = jnp.zeros((rank_count,), jnp.int32).at[destination[1]].set(ranks)
    stored = cache.reshape(rank_count, REQ, PRE, CW)
    prefixes = stored.at[:, REQ - 2].set(stored[source_first, REQ - 2]).at[:, REQ - 1].set(stored[source_second, REQ - 1])
    own_len = prefix_len.reshape(rank_count, REQ)
    lengths = own_len.at[:, REQ - 2].set(own_len[source_first, REQ - 2]).at[:, REQ - 1].set(own_len[source_second, REQ - 1])
    keys_all = jnp.concatenate([prefixes, span_latent.reshape(rank_count, REQ, CHK, CW)], axis=2)
    grouped = queries.reshape(rank_count, REQ, CHK, HEADS, CW)
    scores = jnp.einsum('rjthc,rjkc->rjthk', grouped.astype(jnp.float32), keys_all.astype(jnp.float32)) * score_scale
    allowed = key_mask(lengths, PRE, CHK)[:, :, :, None, :]
    scores = jnp.where(allowed, scores, -jnp.inf)
    highest = lax.optimization_barrier(jnp.max(scores, axis=-1, keepdims=True))
    raised = jnp.exp(scores - highest)
    weights = (raised / lax.optimization_barrier(jnp.sum(raised, axis=-1, keepdims=True))).astype(jnp.bfloat16)
    latent_out = jnp.einsum('rjthk,rjkc->rjthc', weights.astype(jnp.float32), keys_all[..., :LAT].astype(jnp.float32)).astype(jnp.bfloat16)
    latent_out = latent_out.reshape(rank_count * TOK, HEADS, LAT)
    values = jnp.einsum('thc,hcv->thv', latent_out.astype(jnp.float32), uv_weight.astype(jnp.float32)).astype(jnp.bfloat16)
    attended = jnp.dot(values.reshape(rank_count * TOK, HEADS * VH), out_weight, preferred_element_type=jnp.float32)
    mixed_rows = (residual.astype(jnp.float32) + attended).astype(jnp.bfloat16)
    normed = rms_norm(mixed_rows, norm_gain)
    tables = jax.vmap(partial(slot_tables, experts=EXPERTS, capacity=CAPR))
    placer, combiner = tables(routes.reshape(rank_count, TOK, TOPK), route_weight.reshape(rank_count, TOK, TOPK))
    slot_rows = jnp.einsum('rst,rtd->rsd', placer.astype(jnp.float32), normed.reshape(rank_count, TOK, D).astype(jnp.float32)).astype(jnp.bfloat16)
    expert_rows = slot_rows.reshape(rank_count, EXPERTS, CAPR, D).transpose(1, 0, 2, 3).reshape(EXPERTS, rank_count * CAPR, D)

    def expert(operands):
        rows_in, gate_part, up_part, down_part = operands
        gate_proj = jnp.dot(rows_in, gate_part, preferred_element_type=jnp.float32)
        up_proj = jnp.dot(rows_in, up_part, preferred_element_type=jnp.float32)
        hidden = (jax.nn.silu(gate_proj) * up_proj).astype(jnp.bfloat16)
        blocks = hidden.reshape(rows_in.shape[0], members, FF_DEV).astype(jnp.float32)
        pieces = jnp.einsum('rgf,gfd->grd', blocks, down_part.reshape(members, FF_DEV, D).astype(jnp.float32)).astype(jnp.bfloat16)
        return lax.optimization_barrier(jnp.sum(pieces.astype(jnp.float32), axis=0))
    expert_out = lax.map(expert, (expert_rows, gate_weight, up_weight, down_weight))
    returned = expert_out.reshape(EXPERTS, rank_count, CAPR, D).transpose(1, 0, 2, 3).reshape(rank_count, EXPERTS * CAPR, D)
    moe = jnp.einsum('rts,rsd->rtd', combiner.astype(jnp.float32), returned)
    total = mixed_rows.astype(jnp.float32).reshape(rank_count, TOK, D) + moe
    return total.reshape(rank_count * TOK, D).astype(jnp.bfloat16)
```

```python
import jax
import jax.numpy as jnp
from jax import lax
from jax.sharding import Mesh, PartitionSpec as P

score_scale = 192.0 ** (-0.5)
norm_eps = 1e-06
DP = ("dx", "dy")
MEM = ("ep", "tp")
bf16 = jnp.bfloat16
f32 = jnp.float32


def attend(grouped, keys, lengths, prefix_rows, latent_width):
    span_rows = grouped.shape[1]
    scores = jnp.einsum("jthc,jkc->jthk", grouped, keys, preferred_element_type=f32) * score_scale
    key_index = jnp.arange(keys.shape[1], dtype=jnp.int32)
    query_index = jnp.arange(span_rows, dtype=jnp.int32)
    in_prefix = (key_index < prefix_rows) & (key_index < lengths[:, None])
    in_span = (key_index[None, :] >= prefix_rows) & (
        key_index[None, :] - prefix_rows <= query_index[:, None]
    )
    allowed = (in_prefix[:, None, :] | in_span)[:, :, None, :]
    scores = jnp.where(allowed, scores, -jnp.inf)
    highest = jnp.max(scores, axis=-1, keepdims=True)
    raised = jnp.exp(scores - highest)
    weights = (raised / jnp.sum(raised, axis=-1, keepdims=True)).astype(bf16)
    return jnp.einsum(
        "jthk,jkc->jthc", weights, keys[:, :, :latent_width], preferred_element_type=f32
    ).astype(bf16)


def slots_of(route_rows, experts, capacity):
    top_k = route_rows.shape[1]
    flat_routes = route_rows.reshape(-1)
    hits = (flat_routes[:, None] == jnp.arange(experts, dtype=jnp.int32)[None, :]).astype(jnp.int32)
    earlier = jnp.cumsum(hits, axis=0) - hits
    position = jnp.sum(earlier * hits, axis=1)
    return (flat_routes * capacity + position).reshape(-1, top_k).T


def per_device(
    queries,
    cache,
    span_latent,
    prefix_len,
    destination,
    uv_weight,
    out_weight,
    residual,
    norm_gain,
    routes,
    route_weight,
    gate_weight,
    up_weight,
    down_weight,
):
    requests, prefix_rows, cached_width = cache.shape
    span_rows = span_latent.shape[1]
    tok_rows, heads_here = queries.shape[0], queries.shape[1]
    latent_width, value_width = uv_weight.shape[1], uv_weight.shape[2]
    model_width = residual.shape[1]
    nx, ny = lax.axis_size("dx"), lax.axis_size("dy")
    rank_count = nx * ny
    members = lax.axis_size(MEM)
    my_rank = lax.axis_index(DP)
    member = lax.axis_index(MEM)
    core = lax.axis_index("tp")
    col = model_width // members
    core_swap = [(0, 1), (1, 0)]
    swap = [
        (x * members + a * ny + b, a * members + x * ny + b)
        for x in range(nx)
        for a in range(nx)
        for b in range(ny)
    ]
    swap_axes = ("dx", "ep", "tp")

    ranks = jnp.arange(rank_count, dtype=jnp.int32)
    source_first = jnp.sum(ranks * (destination[0] == my_rank).astype(jnp.int32))
    source_second = jnp.sum(ranks * (destination[1] == my_rank).astype(jnp.int32))
    part = prefix_rows // members
    moving = lax.dynamic_slice_in_dim(cache[requests - 2 :], member * part, part, 1)
    arrived = lax.all_to_all(
        jnp.broadcast_to(moving[None], (rank_count,) + moving.shape), DP, 0, 0, tiled=True
    )
    chosen = jnp.stack(
        [
            lax.dynamic_index_in_dim(arrived[:, 0], source_first, 0, keepdims=False),
            lax.dynamic_index_in_dim(arrived[:, 1], source_second, 0, keepdims=False),
        ]
    )
    moved = lax.all_gather(chosen, MEM, axis=1, tiled=True)
    own_len = lax.dynamic_slice_in_dim(prefix_len, my_rank * requests, requests)
    moved_first = lax.dynamic_index_in_dim(prefix_len, source_first * requests + requests - 2, 0)
    moved_second = lax.dynamic_index_in_dim(prefix_len, source_second * requests + requests - 1, 0)

    out_cols = lax.all_gather(out_weight, "dy", axis=0)
    down_cols = lax.all_to_all(
        down_weight[0].reshape(-1, members, col).transpose(1, 0, 2), MEM, 0, 0, tiled=True
    )
    residual_t = lax.ppermute(
        lax.dynamic_slice_in_dim(residual, member * col, col, 1), swap_axes, swap
    )
    capacity = max(2, 3 * tok_rows * routes.shape[1] // (2 * rank_count))
    slots = slots_of(routes, rank_count, capacity)
    slots_t = lax.ppermute(slots, swap_axes, swap)

    grouped = queries.reshape(requests, span_rows, heads_here, cached_width)
    keys_own = jnp.concatenate([cache[: requests - 2], span_latent[: requests - 2]], axis=1)
    keys_moved = jnp.concatenate([moved, span_latent[requests - 2 :]], axis=1)
    latent_own = attend(
        grouped[: requests - 2], keys_own, own_len[: requests - 2], prefix_rows, latent_width
    )
    latent_moved = attend(
        grouped[requests - 2 :],
        keys_moved,
        jnp.concatenate([moved_first, moved_second]),
        prefix_rows,
        latent_width,
    )
    latent_out = jnp.concatenate([latent_own, latent_moved], axis=0)
    latent_out = latent_out.reshape(tok_rows, heads_here, latent_width)
    values = jnp.einsum("thc,hcv->thv", latent_out, uv_weight, preferred_element_type=f32)
    values = values.astype(bf16).reshape(tok_rows, heads_here * value_width)

    values_x = lax.all_gather(values, "dx", axis=0)
    half = ny // 2
    out_cols = out_cols.reshape((half, 2) + out_weight.shape)
    weight_mine = lax.dynamic_index_in_dim(out_cols, core, 1, keepdims=False)
    weight_other = lax.dynamic_index_in_dim(out_cols, 1 - core, 1, keepdims=False)
    sent = jnp.einsum("atk,bkc->abtc", values_x, weight_other, preferred_element_type=f32)
    sent = lax.ppermute(sent.astype(bf16), "tp", core_swap)
    kept = jnp.einsum("atk,bkc->abtc", values_x, weight_mine, preferred_element_type=f32)
    shares = (kept + sent.astype(f32)).astype(bf16).reshape(nx * half, tok_rows, col)
    shares = lax.all_to_all(shares, "ep", 0, 0, tiled=True)
    attended = jnp.sum(shares.astype(f32), axis=0)
    mixed_t = (residual_t.astype(f32) + attended).astype(bf16)
    mixed = lax.ppermute(mixed_t, swap_axes, swap)

    slot_index = jnp.arange(rank_count * capacity, dtype=jnp.int32)
    placer = jnp.any(slot_index[:, None, None] == slots_t[None], axis=1).astype(bf16)
    outgoing = jnp.dot(placer, mixed_t, preferred_element_type=f32).astype(bf16)
    outgoing = outgoing.reshape(rank_count, capacity, col)
    received = lax.all_to_all(outgoing, DP, 0, 0, tiled=True)
    received = received.reshape(nx, ny, capacity, col).transpose(1, 2, 0, 3)
    received = received.reshape(ny * capacity, nx * col)
    rows_in = lax.all_gather(received, MEM, axis=0)
    rows_in = rows_in.reshape(nx, ny, ny * capacity, nx * col)

    gain = norm_gain.astype(f32)[:, None]
    weight_in = jnp.concatenate([gate_weight[0], up_weight[0]], axis=1)
    weight_in = (weight_in.astype(f32) * gain).astype(bf16)
    weight_in = weight_in.reshape(nx, ny, col, -1).transpose(1, 0, 2, 3)
    weight_in = weight_in.reshape(ny, nx * col, -1)
    widened = rows_in.astype(f32)
    mean_square = jnp.sum(widened * widened, axis=(1, 3)) / model_width
    factor = lax.rsqrt(mean_square + norm_eps)[..., None]
    proj = jnp.einsum("abrk,bkf->arf", rows_in, weight_in, preferred_element_type=f32) * factor
    ff = gate_weight.shape[2]
    hidden = (jax.nn.silu(proj[..., :ff]) * proj[..., ff:]).astype(bf16)
    hidden = hidden.reshape(rank_count * capacity, ff)
    hidden_all = lax.all_gather(hidden, MEM, axis=0)
    expert_out = jnp.einsum("mrf,mfc->rc", hidden_all, down_cols, preferred_element_type=f32)
    expert_out = expert_out.astype(bf16).reshape(rank_count, capacity, col)

    returned = lax.all_to_all(expert_out, DP, 0, 0, tiled=True)
    returned = returned.reshape(rank_count * capacity, col)
    matches = slots[:, :, None] == slot_index[None, None, :]
    combiner = jnp.sum(
        jnp.where(matches, route_weight.T[:, :, None], jnp.zeros((), route_weight.dtype)), axis=0
    )
    moe = jnp.dot(combiner, returned, preferred_element_type=f32)
    total = (mixed.astype(f32) + moe).astype(bf16)
    total = lax.all_to_all(total.reshape(members, tok_rows // members, col), MEM, 0, 0, tiled=True)
    return total.transpose(1, 0, 2).reshape(tok_rows // members, model_width)


def solution(mesh):
    dp, ep, tp = mesh.devices.shape
    nx = 1
    while nx * nx < dp:
        nx *= 2
    grid = Mesh(mesh.devices.reshape(nx, dp // nx, ep, tp), DP + MEM)
    in_specs = (
        P(DP, MEM, None),
        P(DP, None, None),
        P(DP, None, None),
        P(),
        P(),
        P(MEM, None, None),
        P(MEM, DP),
        P(DP, None),
        P(),
        P(DP, None),
        P(DP, None),
        P(DP, None, MEM),
        P(DP, None, MEM),
        P(DP, MEM, None),
    )
    out_specs = P(DP + MEM, None)
    return jax.shard_map(
        per_device, mesh=grid, in_specs=in_specs, out_specs=out_specs, check_vma=False
    )
```

```python
import functools

import jax
import jax.numpy as jnp
from jax import lax
from jax.experimental import pallas as pl
from jax.experimental.pallas import tpu as pltpu
from jax.sharding import Mesh, PartitionSpec as P

score_scale = 192.0 ** (-0.5)
norm_eps = 1e-06
DP = ("dx", "dy")
MEM = ("ep", "tp")
bf16 = jnp.bfloat16
f32 = jnp.float32


def attend(grouped, keys, lengths, prefix_rows, latent_width):
    span_rows = grouped.shape[1]
    scores = jnp.einsum("jthc,jkc->jthk", grouped, keys, preferred_element_type=f32) * score_scale
    key_index = jnp.arange(keys.shape[1], dtype=jnp.int32)
    query_index = jnp.arange(span_rows, dtype=jnp.int32)
    in_prefix = (key_index < prefix_rows) & (key_index < lengths[:, None])
    in_span = (key_index[None, :] >= prefix_rows) & (
        key_index[None, :] - prefix_rows <= query_index[:, None]
    )
    allowed = (in_prefix[:, None, :] | in_span)[:, :, None, :]
    scores = jnp.where(allowed, scores, -jnp.inf)
    highest = jnp.max(scores, axis=-1, keepdims=True)
    raised = jnp.exp(scores - highest)
    weights = (raised / jnp.sum(raised, axis=-1, keepdims=True)).astype(bf16)
    return jnp.einsum(
        "jthk,jkc->jthc", weights, keys[:, :, :latent_width], preferred_element_type=f32
    ).astype(bf16)


def slots_of(route_rows, experts, capacity):
    top_k = route_rows.shape[1]
    flat_routes = route_rows.reshape(-1)
    hits = (flat_routes[:, None] == jnp.arange(experts, dtype=jnp.int32)[None, :]).astype(jnp.int32)
    earlier = jnp.cumsum(hits, axis=0) - hits
    position = jnp.sum(earlier * hits, axis=1)
    return (flat_routes * capacity + position).reshape(-1, top_k).T


def share_kernel(core_ref, values_ref, weight_ref, out_ref):
    nx, _, rows, cols = out_ref.shape
    product = jnp.dot(values_ref[...], weight_ref[0], preferred_element_type=f32)
    out_ref[...] = product.astype(bf16).reshape(nx, 1, rows, cols)


def share_sum_kernel(core_ref, values_ref, weight_ref, other_ref, out_ref):
    nx, _, rows, cols = out_ref.shape
    product = jnp.dot(values_ref[...], weight_ref[0], preferred_element_type=f32)
    product = product.reshape(nx, 1, rows, cols) + other_ref[...].astype(f32)
    out_ref[...] = product.astype(bf16)


def project(core, values, weights, other=None):
    blocks, depth, cols = weights.shape
    half = blocks // 2
    total = values.shape[0]
    nx = blocks
    rows = total // nx
    piece = pl.BlockSpec((nx, 1, rows, cols), lambda i, c: (0, i, 0, 0))
    in_specs = [
        pl.BlockSpec((total, depth), lambda i, c: (0, 0)),
        pl.BlockSpec((1, depth, cols), lambda i, c: (2 * i + c[0], 0, 0)),
    ]
    operands = [values, weights]
    if other is not None:
        in_specs.append(piece)
        operands.append(other)
    return pl.pallas_call(
        share_kernel if other is None else share_sum_kernel,
        out_shape=jax.ShapeDtypeStruct((nx, half, rows, cols), bf16),
        grid_spec=pltpu.PrefetchScalarGridSpec(
            num_scalar_prefetch=1, grid=(half,), in_specs=in_specs, out_specs=piece
        ),
        compiler_params=pltpu.CompilerParams(vmem_limit_bytes=32 << 20),
        cost_estimate=pl.CostEstimate(
            flops=2 * total * depth * cols * half,
            bytes_accessed=2 * (total * depth + half * depth * cols + half * total * cols),
            transcendentals=0,
        ),
    )(core, *operands)


def hidden_kernel(width, rows_ref, weight_ref, out_ref, total, squares):
    step = pl.program_id(0)
    groups, _, rows, depth = rows_ref.shape
    block = rows_ref[...].reshape(groups * rows, depth)
    widened = block.astype(f32)
    square = jnp.sum(widened * widened, axis=1, keepdims=True)
    product = jnp.dot(block, weight_ref[0], preferred_element_type=f32)

    @pl.when(step == 0)
    def _():
        total[...] = product
        squares[...] = square

    @pl.when(step > 0)
    def _():
        total[...] += product
        squares[...] += square

    @pl.when(step == pl.num_programs(0) - 1)
    def _():
        factor = lax.rsqrt(squares[...] / width + norm_eps)
        ff = out_ref.shape[1]
        gate = total[:, :ff] * factor
        up = total[:, ff:] * factor
        out_ref[...] = (gate / (1.0 + jnp.exp(-gate)) * up).astype(bf16)


def hidden_of(rows_in, weight_in, width):
    nx, ny, rows, depth = rows_in.shape
    ff2 = weight_in.shape[2]
    return pl.pallas_call(
        functools.partial(hidden_kernel, width),
        out_shape=jax.ShapeDtypeStruct((nx * rows, ff2 // 2), bf16),
        grid=(ny,),
        in_specs=[
            pl.BlockSpec((nx, 1, rows, depth), lambda i: (0, i, 0, 0)),
            pl.BlockSpec((1, depth, ff2), lambda i: (i, 0, 0)),
        ],
        out_specs=pl.BlockSpec((nx * rows, ff2 // 2), lambda i: (0, 0)),
        scratch_shapes=[pltpu.VMEM((nx * rows, ff2), f32), pltpu.VMEM((nx * rows, 1), f32)],
        compiler_params=pltpu.CompilerParams(vmem_limit_bytes=40 << 20),
        cost_estimate=pl.CostEstimate(
            flops=2 * nx * ny * rows * depth * ff2,
            bytes_accessed=2 * (nx * ny * rows * depth + ny * depth * ff2),
            transcendentals=nx * rows * ff2,
        ),
    )(rows_in, weight_in)


def per_device(
    queries,
    cache,
    span_latent,
    prefix_len,
    destination,
    uv_weight,
    out_weight,
    residual,
    norm_gain,
    routes,
    route_weight,
    gate_weight,
    up_weight,
    down_weight,
):
    requests, prefix_rows, cached_width = cache.shape
    span_rows = span_latent.shape[1]
    tok_rows, heads_here = queries.shape[0], queries.shape[1]
    latent_width, value_width = uv_weight.shape[1], uv_weight.shape[2]
    model_width = residual.shape[1]
    nx, ny = lax.axis_size("dx"), lax.axis_size("dy")
    rank_count = nx * ny
    members = lax.axis_size(MEM)
    my_rank = lax.axis_index(DP)
    member = lax.axis_index(MEM)
    core = lax.axis_index("tp")
    col = model_width // members
    core_swap = [(0, 1), (1, 0)]
    swap = [
        (x * members + a * ny + b, a * members + x * ny + b)
        for x in range(nx)
        for a in range(nx)
        for b in range(ny)
    ]
    swap_axes = ("dx", "ep", "tp")

    ranks = jnp.arange(rank_count, dtype=jnp.int32)
    source_first = jnp.sum(ranks * (destination[0] == my_rank).astype(jnp.int32))
    source_second = jnp.sum(ranks * (destination[1] == my_rank).astype(jnp.int32))
    part = prefix_rows // members
    moving = lax.dynamic_slice_in_dim(cache[requests - 2 :], member * part, part, 1)
    arrived = lax.all_to_all(
        jnp.broadcast_to(moving[None], (rank_count,) + moving.shape), DP, 0, 0, tiled=True
    )
    chosen = jnp.stack(
        [
            lax.dynamic_index_in_dim(arrived[:, 0], source_first, 0, keepdims=False),
            lax.dynamic_index_in_dim(arrived[:, 1], source_second, 0, keepdims=False),
        ]
    )
    moved = lax.all_gather(chosen, MEM, axis=1, tiled=True)
    own_len = lax.dynamic_slice_in_dim(prefix_len, my_rank * requests, requests)
    moved_first = lax.dynamic_index_in_dim(prefix_len, source_first * requests + requests - 2, 0)
    moved_second = lax.dynamic_index_in_dim(prefix_len, source_second * requests + requests - 1, 0)

    out_cols = lax.all_gather(out_weight, "dy", axis=0)
    down_cols = lax.all_to_all(
        down_weight[0].reshape(-1, members, col).transpose(1, 0, 2), MEM, 0, 0, tiled=True
    )
    residual_t = lax.ppermute(
        lax.dynamic_slice_in_dim(residual, member * col, col, 1), swap_axes, swap
    )
    capacity = max(2, 3 * tok_rows * routes.shape[1] // (2 * rank_count))
    slots = slots_of(routes, rank_count, capacity)
    slots_t = lax.ppermute(slots, swap_axes, swap)

    gain = norm_gain.astype(f32)[:, None]
    weight_in = jnp.concatenate([gate_weight[0], up_weight[0]], axis=1)
    weight_in = (weight_in.astype(f32) * gain).astype(bf16)
    weight_in = weight_in.reshape(nx, ny, col, -1).transpose(1, 0, 2, 3)
    weight_in = weight_in.reshape(ny, nx * col, -1)

    grouped = queries.reshape(requests, span_rows, heads_here, cached_width)
    keys_own = jnp.concatenate([cache[: requests - 2], span_latent[: requests - 2]], axis=1)
    keys_moved = jnp.concatenate([moved, span_latent[requests - 2 :]], axis=1)
    latent_own = attend(
        grouped[: requests - 2], keys_own, own_len[: requests - 2], prefix_rows, latent_width
    )
    latent_moved = attend(
        grouped[requests - 2 :],
        keys_moved,
        jnp.concatenate([moved_first, moved_second]),
        prefix_rows,
        latent_width,
    )
    latent_out = jnp.concatenate([latent_own, latent_moved], axis=0)
    latent_out = latent_out.reshape(tok_rows, heads_here, latent_width)
    values = jnp.einsum("thc,hcv->thv", latent_out, uv_weight, preferred_element_type=f32)
    values = values.astype(bf16).reshape(tok_rows, heads_here * value_width)

    values_x = lax.all_gather(values, "dx", axis=0).reshape(nx * tok_rows, -1)
    core_at = jnp.reshape(core, (1,))
    sent = lax.ppermute(project(1 - core_at, values_x, out_cols), "tp", core_swap)
    shares = project(core_at, values_x, out_cols, sent).reshape(members // 2, tok_rows, col)
    shares, down_cols, residual_t, slots_t, weight_in = lax.optimization_barrier(
        (shares, down_cols, residual_t, slots_t, weight_in)
    )
    shares = lax.all_to_all(shares, "ep", 0, 0, tiled=True)
    attended = jnp.sum(shares.astype(f32), axis=0)
    mixed_t = (residual_t.astype(f32) + attended).astype(bf16)
    mixed = lax.ppermute(mixed_t, swap_axes, swap)

    slot_index = jnp.arange(rank_count * capacity, dtype=jnp.int32)
    placer = jnp.any(slot_index[:, None, None] == slots_t[None], axis=1).astype(bf16)
    outgoing = jnp.dot(placer, mixed_t, preferred_element_type=f32).astype(bf16)
    outgoing = outgoing.reshape(rank_count, capacity, col)
    received = lax.all_to_all(outgoing, DP, 0, 0, tiled=True)
    received = received.reshape(nx, ny, capacity, col).transpose(1, 2, 0, 3)
    received = received.reshape(ny * capacity, nx * col)
    rows_in = lax.all_gather(received, MEM, axis=0)
    rows_in = rows_in.reshape(nx, ny, ny * capacity, nx * col)

    hidden = hidden_of(rows_in, weight_in, float(model_width))
    hidden_all = lax.all_gather(hidden, MEM, axis=0)
    expert_out = jnp.einsum("mrf,mfc->rc", hidden_all, down_cols, preferred_element_type=f32)
    expert_out = expert_out.astype(bf16).reshape(rank_count, capacity, col)

    returned = lax.all_to_all(expert_out, DP, 0, 0, tiled=True)
    returned = returned.reshape(rank_count * capacity, col)
    matches = slots[:, :, None] == slot_index[None, None, :]
    combiner = jnp.sum(
        jnp.where(matches, route_weight.T[:, :, None], jnp.zeros((), route_weight.dtype)), axis=0
    )
    moe = jnp.dot(combiner, returned, preferred_element_type=f32)
    total = (mixed.astype(f32) + moe).astype(bf16)
    total = lax.all_to_all(total.reshape(members, tok_rows // members, col), MEM, 0, 0, tiled=True)
    return total.transpose(1, 0, 2).reshape(tok_rows // members, model_width)


def solution(mesh):
    dp, ep, tp = mesh.devices.shape
    nx = 1
    while nx * nx < dp:
        nx *= 2
    grid = Mesh(mesh.devices.reshape(nx, dp // nx, ep, tp), DP + MEM)
    in_specs = (
        P(DP, MEM, None),
        P(DP, None, None),
        P(DP, None, None),
        P(),
        P(),
        P(MEM, None, None),
        P(MEM, DP),
        P(DP, None),
        P(),
        P(DP, None),
        P(DP, None),
        P(DP, None, MEM),
        P(DP, None, MEM),
        P(DP, MEM, None),
    )
    out_specs = P(DP + MEM, None)
    return jax.shard_map(
        per_device, mesh=grid, in_specs=in_specs, out_specs=out_specs, check_vma=False
    )
```

```python
import functools

import jax
import jax.numpy as jnp
from jax import lax
from jax.experimental import pallas as pl
from jax.experimental.pallas import tpu as pltpu
from jax.sharding import Mesh, PartitionSpec as P

score_scale = 192.0 ** (-0.5)
norm_eps = 1e-06
DP = ("dx", "dy")
MEM = ("ep", "tp")
SWAP = ("dx", "ep", "tp")
bf16 = jnp.bfloat16
f32 = jnp.float32
VMEM_LIMIT = 56 << 20
NT = (((1,), (1,)), ((), ()))


def params():
    return pltpu.CompilerParams(vmem_limit_bytes=VMEM_LIMIT)


def cost(flops, nbytes):
    return pl.CostEstimate(flops=flops, bytes_accessed=nbytes, transcendentals=0)


def attend_kernel(lengths_ref, query_ref, prefix_ref, span_ref, uv_ref, out_ref):
    step = pl.program_id(0)
    length = lengths_ref[step]
    span_rows, heads, width = query_ref.shape
    latent, value = uv_ref.shape[1], uv_ref.shape[2]
    span = span_ref[0]
    prefix = prefix_ref[...].reshape(-1, width)
    prefix_rows = prefix.shape[0]
    rows = jnp.concatenate([query_ref[:, h, :] for h in range(heads)], axis=0)
    first = lax.dot_general(rows, prefix, NT, preferred_element_type=f32) * score_scale
    second = lax.dot_general(rows, span, NT, preferred_element_type=f32) * score_scale
    total = heads * span_rows
    key = lax.broadcasted_iota(jnp.int32, (total, prefix_rows), 1)
    first = jnp.where(key < length, first, -jnp.inf)
    token = lax.rem(lax.broadcasted_iota(jnp.int32, (total, span_rows), 0), span_rows)
    late = lax.broadcasted_iota(jnp.int32, (total, span_rows), 1)
    second = jnp.where(late <= token, second, -jnp.inf)
    highest = jnp.maximum(
        jnp.max(first, axis=1, keepdims=True), jnp.max(second, axis=1, keepdims=True)
    )
    first = jnp.exp(first - highest)
    second = jnp.exp(second - highest)
    norm = jnp.sum(first, axis=1, keepdims=True) + jnp.sum(second, axis=1, keepdims=True)
    out = jnp.dot((first / norm).astype(bf16), prefix[:, :latent], preferred_element_type=f32)
    out += jnp.dot((second / norm).astype(bf16), span[:, :latent], preferred_element_type=f32)
    out = out.astype(bf16)
    for h in range(heads):
        part = jnp.dot(
            out[h * span_rows : (h + 1) * span_rows], uv_ref[h], preferred_element_type=f32
        )
        out_ref[:, h * value : (h + 1) * value] = part.astype(bf16)


def attend(lengths, queries, prefix, prefix_spec, span, uv_weight, first_request, count):
    span_rows, width = span.shape[1], span.shape[2]
    heads = queries.shape[1]
    latent, value = uv_weight.shape[1], uv_weight.shape[2]
    keys = 288
    return pl.pallas_call(
        attend_kernel,
        out_shape=jax.ShapeDtypeStruct((count * span_rows, heads * value), bf16),
        grid_spec=pltpu.PrefetchScalarGridSpec(
            num_scalar_prefetch=1,
            grid=(count,),
            in_specs=[
                pl.BlockSpec((span_rows, heads, width), lambda j, n: (first_request + j, 0, 0)),
                prefix_spec,
                pl.BlockSpec((1, span_rows, width), lambda j, n: (first_request + j, 0, 0)),
                pl.BlockSpec((heads, latent, value), lambda j, n: (0, 0, 0)),
            ],
            out_specs=pl.BlockSpec((span_rows, heads * value), lambda j, n: (j, 0)),
        ),
        compiler_params=params(),
        cost_estimate=cost(
            2 * count * span_rows * heads * (keys * (width + latent) + latent * value),
            2 * count * (span_rows * heads * width + keys * width) + 2 * heads * latent * value,
        ),
    )(lengths, queries, prefix, span, uv_weight)


def share_kernel(core_ref, values_ref, weight_ref, *refs):
    out_ref = refs[-1]
    nx, _, cols, rows = out_ref.shape
    contract = (((0,), (1,)), ((), ()))
    for a in range(nx):
        piece = lax.dot_general(
            weight_ref[0], values_ref[a], contract, preferred_element_type=f32
        )
        if len(refs) == 2:
            piece += refs[0][a, 0].astype(f32)
        out_ref[a, 0] = piece.astype(bf16)


def project(core, values, weights, *other):
    nx, rows, depth = values.shape
    blocks, _, cols = weights.shape
    half = blocks // 2
    piece = pl.BlockSpec((nx, 1, cols, rows), lambda i, c: (0, i, 0, 0))
    return pl.pallas_call(
        share_kernel,
        out_shape=jax.ShapeDtypeStruct((nx, half, cols, rows), bf16),
        grid_spec=pltpu.PrefetchScalarGridSpec(
            num_scalar_prefetch=1,
            grid=(half,),
            in_specs=[
                pl.BlockSpec((nx, rows, depth), lambda i, c: (0, 0, 0)),
                pl.BlockSpec((1, depth, cols), lambda i, c: (2 * i + c[0], 0, 0)),
            ]
            + [piece] * len(other),
            out_specs=piece,
        ),
        compiler_params=params(),
        cost_estimate=cost(
            2 * nx * rows * depth * cols * half,
            2 * (nx * rows * depth + half * depth * cols + half * nx * rows * cols),
        ),
    )(core, values, weights, *other)


def hidden_kernel(width, rows_ref, gain_ref, gate_ref, up_ref, out_ref, total, squares):
    step = pl.program_id(0)
    groups, _, rows, depth = rows_ref.shape
    block = rows_ref[...].reshape(groups * rows, depth)
    widened = block.astype(f32)
    square = jnp.sum(widened * widened, axis=1, keepdims=True)
    scaled = (widened * gain_ref[0]).astype(bf16)
    gate = gate_ref[...].reshape(depth, -1)
    up = up_ref[...].reshape(depth, -1)
    weight = jnp.concatenate([gate, up], axis=1)
    product = jnp.dot(scaled, weight, preferred_element_type=f32)

    @pl.when(step == 0)
    def _():
        total[...] = product
        squares[...] = square

    @pl.when(step > 0)
    def _():
        total[...] += product
        squares[...] += square

    @pl.when(step == pl.num_programs(0) - 1)
    def _():
        factor = lax.rsqrt(squares[...] / width + norm_eps)
        ff = out_ref.shape[1]
        gate = total[:, :ff] * factor
        up = total[:, ff:] * factor
        out_ref[...] = (gate / (1.0 + jnp.exp(-gate)) * up).astype(bf16)


def hidden_of(rows_in, gain, gate_weight, up_weight, width):
    nx, ny, rows, depth = rows_in.shape
    ff = gate_weight.shape[3]
    weight_spec = pl.BlockSpec((nx, 1, depth // nx, ff), lambda i: (0, i, 0, 0))
    return pl.pallas_call(
        functools.partial(hidden_kernel, width),
        out_shape=jax.ShapeDtypeStruct((nx * rows, ff), bf16),
        grid=(ny,),
        in_specs=[
            pl.BlockSpec((nx, 1, rows, depth), lambda i: (0, i, 0, 0)),
            pl.BlockSpec((1, 1, depth), lambda i: (i, 0, 0)),
            weight_spec,
            weight_spec,
        ],
        out_specs=pl.BlockSpec((nx * rows, ff), lambda i: (0, 0)),
        scratch_shapes=[pltpu.VMEM((nx * rows, 2 * ff), f32), pltpu.VMEM((nx * rows, 1), f32)],
        compiler_params=params(),
        cost_estimate=cost(
            4 * nx * ny * rows * depth * ff, 2 * (nx * ny * rows * depth + 2 * ny * depth * ff)
        ),
    )(rows_in, gain, gate_weight, up_weight)


def places_of(route_rows, experts):
    flat_routes = route_rows.reshape(-1)
    hits = (flat_routes[:, None] == jnp.arange(experts, dtype=jnp.int32)[None, :]).astype(jnp.int32)
    earlier = jnp.cumsum(hits, axis=0) - hits
    return jnp.sum(earlier * hits, axis=1).reshape(route_rows.shape)


def per_device(
    queries,
    cache,
    span_latent,
    prefix_len,
    destination,
    uv_weight,
    out_weight,
    residual,
    norm_gain,
    routes,
    route_weight,
    gate_weight,
    up_weight,
    down_weight,
):
    requests, prefix_rows, cached_width = cache.shape
    tok_rows = queries.shape[0]
    model_width = residual.shape[1]
    top_k = routes.shape[1]
    ff = gate_weight.shape[2]
    nx, ny = lax.axis_size("dx"), lax.axis_size("dy")
    nz = lax.axis_size("ep")
    rank_count = nx * ny
    members = lax.axis_size(MEM)
    my_rank = lax.axis_index(DP)
    member = lax.axis_index(MEM)
    layer = lax.axis_index("ep")
    core = lax.axis_index("tp")
    col = model_width // members
    capacity = max(2, 3 * tok_rows * top_k // (2 * rank_count))
    swap = [
        (x * members + a * ny + b, a * members + x * ny + b)
        for x in range(nx)
        for a in range(nx)
        for b in range(ny)
    ]

    def other_core(array):
        return lax.ppermute(array, "tp", [(0, 1), (1, 0)])

    def along(array, hops):
        return lax.ppermute(array, "ep", [(z, (z + hops) % nz) for z in range(nz)])

    ranks = jnp.arange(rank_count, dtype=jnp.int32)
    source_first = jnp.sum(ranks * (destination[0] == my_rank).astype(jnp.int32))
    source_second = jnp.sum(ranks * (destination[1] == my_rank).astype(jnp.int32))
    part = prefix_rows // members
    moving = lax.dynamic_slice_in_dim(cache[requests - 2 :], member * part, part, 1)
    arrived = lax.all_to_all(
        jnp.broadcast_to(moving[None], (rank_count,) + moving.shape), DP, 0, 0, tiled=True
    )
    chosen = jnp.stack(
        [
            lax.dynamic_index_in_dim(arrived[:, 0], source_first, 0, keepdims=False),
            lax.dynamic_index_in_dim(arrived[:, 1], source_second, 0, keepdims=False),
        ]
    )
    moved = lax.all_gather(chosen, MEM, axis=0)
    own_len = lax.dynamic_slice_in_dim(prefix_len, my_rank * requests, requests - 2)
    moved_len = jnp.concatenate(
        [
            lax.dynamic_slice_in_dim(prefix_len, source_first * requests + requests - 2, 1),
            lax.dynamic_slice_in_dim(prefix_len, source_second * requests + requests - 1, 1),
        ]
    )

    out_cols = lax.all_gather(out_weight, "dy", axis=0)
    down_t = down_weight[0].T.reshape(nz, 2, col, ff)
    down_mine = lax.dynamic_index_in_dim(down_t, core, 1, keepdims=False)
    down_other = other_core(lax.dynamic_index_in_dim(down_t, 1 - core, 1, keepdims=False))
    down_pair = jnp.stack([down_mine, down_other], axis=1)

    def down_for(hops):
        piece = lax.dynamic_index_in_dim(down_pair, lax.rem(layer + hops, nz), 0, keepdims=False)
        return along(piece, hops) if hops else piece

    hop_order = list(range(nz))
    down_parts = [down_for(hops) for hops in hop_order]
    places = places_of(routes, rank_count)
    packed = jnp.concatenate(
        [
            lax.dynamic_slice_in_dim(residual, member * col, col, 1).T,
            routes.T.astype(bf16),
            places.T.astype(bf16),
            jnp.zeros((16 - 2 * top_k, tok_rows), bf16),
        ],
        axis=0,
    )
    packed_t = lax.ppermute(packed, SWAP, swap)

    part_rows = cache.shape[1]
    values_own = attend(
        own_len,
        queries,
        cache,
        pl.BlockSpec((1, part_rows, cached_width), lambda j, n: (j, 0, 0)),
        span_latent,
        uv_weight,
        0,
        requests - 2,
    )
    values_moved = attend(
        moved_len,
        queries,
        moved,
        pl.BlockSpec((members, 1, part, cached_width), lambda j, n: (0, j, 0, 0)),
        span_latent,
        uv_weight,
        requests - 2,
        2,
    )
    values = jnp.concatenate([values_own, values_moved], axis=0)

    values_x = lax.all_gather(values, "dx", axis=0)
    core_at = jnp.reshape(core, (1,))
    sent = other_core(project(1 - core_at, values_x, out_cols))
    shares = project(core_at, values_x, out_cols, sent).reshape(nz, col, tok_rows)
    shares, down_parts, packed_t = lax.optimization_barrier((shares, down_parts, packed_t))
    shares = lax.all_to_all(shares, "ep", 0, 0, tiled=True)
    attended = jnp.sum(shares.astype(f32), axis=0)
    mixed_t = (packed_t[:col].astype(f32) + attended).astype(bf16)
    mixed = lax.ppermute(mixed_t, SWAP, swap)

    slot_index = jnp.arange(rank_count * capacity, dtype=jnp.int32)
    routes_t = packed_t[col : col + top_k].astype(jnp.int32)
    places_t = packed_t[col + top_k : col + 2 * top_k].astype(jnp.int32)
    slots_t = routes_t * capacity + places_t
    placer = jnp.any(slot_index[:, None, None] == slots_t[None], axis=1).astype(bf16)
    outgoing = lax.dot_general(placer, mixed_t, NT, preferred_element_type=f32).astype(bf16)
    outgoing = outgoing.reshape(rank_count, capacity, col)
    received = lax.all_to_all(outgoing, DP, 0, 0, tiled=True)
    received = received.reshape(nx, ny, capacity, col).transpose(1, 2, 0, 3)
    received = received.reshape(ny * capacity, nx * col)
    rows_in = lax.all_gather(received, MEM, axis=0)
    rows_in, mixed = lax.optimization_barrier((rows_in, mixed))
    rows_in = rows_in.reshape(nx, ny, ny * capacity, nx * col)
    gain = norm_gain.astype(f32).reshape(nx, ny, col).transpose(1, 0, 2).reshape(ny, 1, nx * col)
    hidden = hidden_of(
        rows_in,
        gain,
        gate_weight.reshape(nx, ny, col, ff),
        up_weight.reshape(nx, ny, col, ff),
        float(model_width),
    )

    half = hidden.shape[0] // 2
    blocks = {0: hidden}
    up_way, down_way = hidden, hidden
    for hops in range(1, nz // 2):
        up_way, down_way = along(up_way, 1), along(down_way, -1)
        blocks[hops], blocks[nz - hops] = up_way, down_way
    blocks[nz // 2] = jnp.concatenate([along(up_way[:half], 1), along(down_way[half:], -1)], axis=0)
    hidden_all = jnp.stack([jnp.stack([blocks[h], other_core(blocks[h])]) for h in hop_order])
    down_all = jnp.stack(down_parts)
    expert_out = jnp.einsum("dsrf,dscf->rc", hidden_all, down_all, preferred_element_type=f32)
    expert_out = expert_out.astype(bf16).reshape(rank_count, capacity, col)

    returned = lax.all_to_all(expert_out, DP, 0, 0, tiled=True)
    returned = returned.reshape(rank_count * capacity, col)
    slots = (routes * capacity + places).T
    matches = slots[:, :, None] == slot_index[None, None, :]
    combiner = jnp.sum(
        jnp.where(matches, route_weight.T[:, :, None], jnp.zeros((), route_weight.dtype)), axis=0
    )
    moe = jnp.dot(combiner, returned, preferred_element_type=f32)
    total = (mixed.T.astype(f32) + moe).astype(bf16)
    total = lax.all_to_all(total.reshape(members, tok_rows // members, col), MEM, 0, 0, tiled=True)
    return total.transpose(1, 0, 2).reshape(tok_rows // members, model_width)


def solution(mesh):
    dp, ep, tp = mesh.devices.shape
    nx = 1
    while nx * nx < dp:
        nx *= 2
    grid = Mesh(mesh.devices.reshape(nx, dp // nx, ep, tp), DP + MEM)
    in_specs = (
        P(DP, MEM, None),
        P(DP, None, None),
        P(DP, None, None),
        P(),
        P(),
        P(MEM, None, None),
        P(MEM, DP),
        P(DP, None),
        P(),
        P(DP, None),
        P(DP, None),
        P(DP, None, MEM),
        P(DP, None, MEM),
        P(DP, MEM, None),
    )
    out_specs = P(DP + MEM, None)
    return jax.shard_map(
        per_device, mesh=grid, in_specs=in_specs, out_specs=out_specs, check_vma=False
    )
```

```python
import functools

import jax
import jax.numpy as jnp
from jax import lax
from jax.experimental import pallas as pl
from jax.experimental.pallas import tpu as pltpu
from jax.sharding import Mesh, PartitionSpec as P

score_scale = 192.0 ** (-0.5)
norm_eps = 1e-06
DP = ("dx", "dy")
MEM = ("ep", "tp")
SWAP = ("dx", "ep", "tp")
bf16 = jnp.bfloat16
f32 = jnp.float32
VMEM_LIMIT = 56 << 20
NN = (((1,), (0,)), ((), ()))
NT = (((1,), (1,)), ((), ()))


def params():
    return pltpu.CompilerParams(vmem_limit_bytes=VMEM_LIMIT)


def cost(flops, nbytes):
    return pl.CostEstimate(flops=flops, bytes_accessed=nbytes, transcendentals=0)


def attend_one(rows, length, prefix, prefix_dims, span, uv_ref, latent, store):
    total, span_rows = rows.shape[0], span.shape[0]
    keys_first = prefix_dims is NT
    cached = prefix[:, :latent] if keys_first else prefix[:latent]
    first = lax.dot_general(rows, prefix, prefix_dims, preferred_element_type=f32) * score_scale
    second = lax.dot_general(rows, span, NT, preferred_element_type=f32) * score_scale
    key = lax.broadcasted_iota(jnp.int32, first.shape, 1)
    first = jnp.where(key < length, first, -jnp.inf)
    token = lax.rem(lax.broadcasted_iota(jnp.int32, second.shape, 0), span_rows)
    late = lax.broadcasted_iota(jnp.int32, second.shape, 1)
    second = jnp.where(late <= token, second, -jnp.inf)
    highest = jnp.maximum(
        jnp.max(first, axis=1, keepdims=True), jnp.max(second, axis=1, keepdims=True)
    )
    first = jnp.exp(first - highest)
    second = jnp.exp(second - highest)
    norm = jnp.sum(first, axis=1, keepdims=True) + jnp.sum(second, axis=1, keepdims=True)
    first = (first / norm).astype(bf16)
    second = (second / norm).astype(bf16)
    out = lax.dot_general(first, cached, NN if keys_first else NT, preferred_element_type=f32)
    out += jnp.dot(second, span[:, :latent], preferred_element_type=f32)
    out = out.astype(bf16)
    for h in range(total // span_rows):
        part = jnp.dot(
            out[h * span_rows : (h + 1) * span_rows], uv_ref[h], preferred_element_type=f32
        )
        store(h, part.astype(bf16))


def own_kernel(lengths_ref, query_ref, prefix_ref, span_ref, uv_ref, out_ref, rows_ref):
    heads, latent, value = uv_ref.shape
    span_rows = span_ref.shape[1]
    here = prefix_ref.shape[0]
    turned = [query_ref[h].T for h in range(heads)]
    for j in range(here + rows_ref.shape[0]):
        at = slice(j * span_rows, (j + 1) * span_rows)
        rows = jnp.concatenate([turned[h][at] for h in range(heads)], axis=0)
        if j >= here:
            rows_ref[j - here] = rows
            continue

        def store(h, part):
            out_ref[at, h * value : (h + 1) * value] = part

        attend_one(rows, lengths_ref[j], prefix_ref[j], NN, span_ref[j], uv_ref, latent, store)


def moved_kernel(lengths_ref, rows_ref, prefix_ref, span_ref, uv_ref, out_ref):
    heads, latent, value = uv_ref.shape
    here, _, width = rows_ref.shape
    span_rows = span_ref.shape[1]
    for j in range(here):
        at = slice(j * span_rows, (j + 1) * span_rows)

        def store(h, part):
            out_ref[at, h * value : (h + 1) * value] = part

        prefix = prefix_ref[:, j].reshape(-1, width)
        attend_one(rows_ref[j], lengths_ref[j], prefix, NT, span_ref[j], uv_ref, latent, store)


def attend_call(kernel, operands, specs, shapes):
    flops = 2 * 2 * 128 * (288 * (576 + 512) + 512 * 128)
    outs = [jax.ShapeDtypeStruct(shape, bf16) for shape in shapes]
    return pl.pallas_call(
        kernel,
        out_shape=outs,
        in_specs=[pl.BlockSpec(memory_space=pltpu.SMEM)] + specs,
        out_specs=[whole(shape) for shape in shapes],
        grid=(1,),
        compiler_params=params(),
        cost_estimate=cost(flops, 2 << 20),
    )(*operands)


def whole(shape, block=0):
    return pl.BlockSpec(tuple(shape), lambda i: (block,) + (0,) * (len(shape) - 1))


def share_kernel(core_ref, values_ref, weight_ref, *refs):
    out_ref = refs[-1]
    nx, _, cols, rows = out_ref.shape
    for a in range(nx):
        piece = lax.dot_general(
            weight_ref[0], values_ref[a], NT, preferred_element_type=f32
        )
        if len(refs) == 2:
            piece += refs[0][a, 0].astype(f32)
        out_ref[a, 0] = piece.astype(bf16)


def project(core, values, weights, *other):
    nx, rows, depth = values.shape
    blocks, cols, _ = weights.shape
    half = blocks // 2
    piece = pl.BlockSpec((nx, 1, cols, rows), lambda i, c: (0, i, 0, 0))
    return pl.pallas_call(
        share_kernel,
        out_shape=jax.ShapeDtypeStruct((nx, half, cols, rows), bf16),
        grid_spec=pltpu.PrefetchScalarGridSpec(
            num_scalar_prefetch=1,
            grid=(half,),
            in_specs=[
                pl.BlockSpec((nx, rows, depth), lambda i, c: (0, 0, 0)),
                pl.BlockSpec((1, cols, depth), lambda i, c: (2 * i + c[0], 0, 0)),
            ]
            + [piece] * len(other),
            out_specs=piece,
        ),
        compiler_params=params(),
        cost_estimate=cost(
            2 * nx * rows * depth * cols * half,
            2 * (nx * rows * depth + half * depth * cols + half * nx * rows * cols),
        ),
    )(core, values, weights, *other)


def hidden_kernel(width, rows_ref, gain_ref, gate_ref, up_ref, out_ref, total, squares):
    step = pl.program_id(0)
    groups, _, rows, depth = rows_ref.shape
    block = rows_ref[...].reshape(groups * rows, depth)
    widened = block.astype(f32)
    square = jnp.sum(widened * widened, axis=1, keepdims=True)
    scaled = (widened * gain_ref[0]).astype(bf16)
    gate = gate_ref[...].reshape(depth, -1)
    up = up_ref[...].reshape(depth, -1)
    weight = jnp.concatenate([gate, up], axis=1)
    product = jnp.dot(scaled, weight, preferred_element_type=f32)

    @pl.when(step == 0)
    def _():
        total[...] = product
        squares[...] = square

    @pl.when(step > 0)
    def _():
        total[...] += product
        squares[...] += square

    @pl.when(step == pl.num_programs(0) - 1)
    def _():
        factor = lax.rsqrt(squares[...] / width + norm_eps)
        ff = out_ref.shape[1]
        gate = total[:, :ff] * factor
        up = total[:, ff:] * factor
        out_ref[...] = (gate / (1.0 + jnp.exp(-gate)) * up).astype(bf16)


def hidden_of(rows_in, gain, gate_weight, up_weight, width):
    nx, ny, rows, depth = rows_in.shape
    ff = gate_weight.shape[3]
    weight_spec = pl.BlockSpec((nx, 1, depth // nx, ff), lambda i: (0, i, 0, 0))
    return pl.pallas_call(
        functools.partial(hidden_kernel, width),
        out_shape=jax.ShapeDtypeStruct((nx * rows, ff), bf16),
        grid=(ny,),
        in_specs=[
            pl.BlockSpec((nx, 1, rows, depth), lambda i: (0, i, 0, 0)),
            pl.BlockSpec((1, 1, depth), lambda i: (i, 0, 0)),
            weight_spec,
            weight_spec,
        ],
        out_specs=pl.BlockSpec((nx * rows, ff), lambda i: (0, 0)),
        scratch_shapes=[pltpu.VMEM((nx * rows, 2 * ff), f32), pltpu.VMEM((nx * rows, 1), f32)],
        compiler_params=params(),
        cost_estimate=cost(
            4 * nx * ny * rows * depth * ff, 2 * (nx * ny * rows * depth + 2 * ny * depth * ff)
        ),
    )(rows_in, gain, gate_weight, up_weight)


def slices_kernel(layer_ref, in_ref, *out_refs):
    step = pl.program_id(0)
    for hops, out_ref in enumerate(out_refs):

        @pl.when(step == hops)
        def _(out_ref=out_ref):
            out_ref[...] = in_ref[...]


def slices_of(layer, array, count):
    rows, columns = array.shape
    width = columns // count
    return pl.pallas_call(
        slices_kernel,
        out_shape=[jax.ShapeDtypeStruct((rows, width), array.dtype)] * count,
        grid_spec=pltpu.PrefetchScalarGridSpec(
            num_scalar_prefetch=1,
            grid=(count,),
            in_specs=[pl.BlockSpec((rows, width), lambda i, z: (0, lax.rem(z[0] + i, count)))],
            out_specs=[pl.BlockSpec((rows, width), lambda i, z: (0, 0))] * count,
        ),
        compiler_params=params(),
        cost_estimate=cost(0, 4 * rows * columns),
    )(layer, array)


def down_kernel(core_ref, *refs):
    count = (len(refs) - 2) // 2
    kept_ref, sent_ref = refs[-2:]
    total = None
    for hidden_ref, weight_ref in zip(refs[:count], refs[count : 2 * count]):
        product = jnp.dot(hidden_ref[...], weight_ref[...], preferred_element_type=f32)
        total = product if total is None else total + product
    col = kept_ref.shape[1]
    low, high = total[:, :col], total[:, col:]
    first = core_ref[0] == 0
    kept_ref[...] = jnp.where(first, low, high)
    sent_ref[...] = jnp.where(first, high, low).astype(bf16)


def down_project(core, hidden, weights):
    rows = hidden[0].shape[0]
    cols = weights[0].shape[1] // 2
    operands = list(hidden) + list(weights)
    return pl.pallas_call(
        down_kernel,
        out_shape=[
            jax.ShapeDtypeStruct((rows, cols), f32),
            jax.ShapeDtypeStruct((rows, cols), bf16),
        ],
        grid=(1,),
        in_specs=[pl.BlockSpec(memory_space=pltpu.SMEM)] + [whole(o.shape) for o in operands],
        out_specs=[whole((rows, cols))] * 2,
        compiler_params=params(),
        cost_estimate=cost(4 * rows * cols * 1024, 5 << 20),
    )(core, *operands)


def places_of(route_rows, experts):
    flat_routes = route_rows.reshape(-1)
    hits = (flat_routes[:, None] == jnp.arange(experts, dtype=jnp.int32)[None, :]).astype(jnp.int32)
    earlier = jnp.cumsum(hits, axis=0) - hits
    return jnp.sum(earlier * hits, axis=1).reshape(route_rows.shape)


def per_device(
    queries,
    cache,
    span_latent,
    prefix_len,
    destination,
    uv_weight,
    out_weight,
    residual,
    norm_gain,
    routes,
    route_weight,
    gate_weight,
    up_weight,
    down_weight,
):
    requests, prefix_rows, cached_width = cache.shape
    tok_rows = queries.shape[0]
    model_width = residual.shape[1]
    top_k = routes.shape[1]
    ff = gate_weight.shape[2]
    nx, ny = lax.axis_size("dx"), lax.axis_size("dy")
    nz = lax.axis_size("ep")
    rank_count = nx * ny
    members = lax.axis_size(MEM)
    my_rank = lax.axis_index(DP)
    member = lax.axis_index(MEM)
    layer = lax.axis_index("ep")
    core = lax.axis_index("tp")
    col = model_width // members
    capacity = max(2, 3 * tok_rows * top_k // (2 * rank_count))
    swap = [
        (x * members + a * ny + b, a * members + x * ny + b)
        for x in range(nx)
        for a in range(nx)
        for b in range(ny)
    ]

    def other_core(array):
        return lax.ppermute(array, "tp", [(0, 1), (1, 0)])

    def along(array, hops):
        return lax.ppermute(array, "ep", [(z, (z + hops) % nz) for z in range(nz)])

    ranks = jnp.arange(rank_count, dtype=jnp.int32)
    source_first = jnp.sum(ranks * (destination[0] == my_rank).astype(jnp.int32))
    source_second = jnp.sum(ranks * (destination[1] == my_rank).astype(jnp.int32))
    part = prefix_rows // members
    moving = lax.dynamic_slice_in_dim(cache[requests - 2 :], member * part, part, 1)
    arrived = lax.all_to_all(
        jnp.broadcast_to(moving[None], (rank_count,) + moving.shape), DP, 0, 0, tiled=True
    )
    own_len = lax.dynamic_slice_in_dim(prefix_len, my_rank * requests, requests - 2)
    moved_len = jnp.concatenate(
        [
            lax.dynamic_slice_in_dim(prefix_len, source_first * requests + requests - 2, 1),
            lax.dynamic_slice_in_dim(prefix_len, source_second * requests + requests - 1, 1),
        ]
    )

    out_cols = lax.all_gather(out_weight.T, "dy", axis=0)
    slices = slices_of(jnp.reshape(layer, (1,)), down_weight[0], nz)
    places = places_of(routes, rank_count)
    packed = jnp.concatenate(
        [
            lax.dynamic_slice_in_dim(residual, member * col, col, 1).T,
            routes.T.astype(bf16),
            places.T.astype(bf16),
            jnp.zeros((16 - 2 * top_k, tok_rows), bf16),
        ],
        axis=0,
    )
    packed_t = lax.ppermute(packed, SWAP, swap)

    down = {0: slices[0], 3: along(slices[3], 3), nz - 3: along(slices[nz - 3], -3)}
    arrived, down[3], down[nz - 3] = lax.optimization_barrier((arrived, down[3], down[nz - 3]))
    chosen = jnp.stack(
        [
            lax.dynamic_index_in_dim(arrived[:, 0], source_first, 0, keepdims=False),
            lax.dynamic_index_in_dim(arrived[:, 1], source_second, 0, keepdims=False),
        ]
    )
    moved = lax.all_gather(chosen, MEM, axis=0)

    heads, latent = queries.shape[1], uv_weight.shape[1]
    value = uv_weight.shape[2]
    here = requests - 2
    span_rows = span_latent.shape[1]
    values_shape = (2 * span_rows, heads * value)
    turned = (queries.transpose(1, 2, 0), cache.transpose(0, 2, 1))
    spans = (2, span_rows, cached_width)
    values_own, query_rows = attend_call(
        own_kernel,
        (own_len, *turned, span_latent, uv_weight),
        [
            whole(turned[0].shape),
            whole((here, cached_width, prefix_rows)),
            whole(spans),
            whole(uv_weight.shape),
        ],
        [values_shape, (2, heads * span_rows, cached_width)],
    )
    (values_moved,) = attend_call(
        moved_kernel,
        (moved_len, query_rows, moved, span_latent, uv_weight),
        [whole(query_rows.shape), whole(moved.shape), whole(spans, 1), whole(uv_weight.shape)],
        [values_shape],
    )
    values = jnp.concatenate([values_own, values_moved], axis=0)

    middle = nz // 2
    rows_half = ff // 2
    second = [slices[middle], slices[1], slices[nz - 1]]
    second, _ = lax.optimization_barrier((second, moved))
    second = [
        along(second[0][:rows_half], middle),
        along(second[0][rows_half:], -middle),
        along(second[1], 1),
        along(second[2], -1),
    ]

    values_x = lax.all_gather(values, "dx", axis=0)
    core_at = jnp.reshape(core, (1,))
    sent = other_core(project(1 - core_at, values_x, out_cols))
    shares = project(core_at, values_x, out_cols, sent).reshape(nz, col, tok_rows)
    shares, second, packed_t = lax.optimization_barrier((shares, second, packed_t))
    down[middle] = jnp.concatenate(second[:2], axis=0)
    down[1], down[nz - 1] = second[2:]
    shares = lax.all_to_all(shares, "ep", 0, 0, tiled=True)
    attended = jnp.sum(shares.astype(f32), axis=0)
    mixed_t = (packed_t[:col].astype(f32) + attended).astype(bf16)
    mixed = lax.ppermute(mixed_t, SWAP, swap)

    third = [slices[2], slices[nz - 2]]
    third, mixed_t = lax.optimization_barrier((third, mixed_t))
    third = [along(third[0], 2), along(third[1], -2)]

    slot_index = jnp.arange(rank_count * capacity, dtype=jnp.int32)
    routes_t = packed_t[col : col + top_k].astype(jnp.int32)
    places_t = packed_t[col + top_k : col + 2 * top_k].astype(jnp.int32)
    slots_t = routes_t * capacity + places_t
    placer = jnp.any(slot_index[:, None, None] == slots_t[None], axis=1).astype(bf16)
    outgoing = lax.dot_general(placer, mixed_t, NT, preferred_element_type=f32).astype(bf16)
    outgoing = outgoing.reshape(rank_count, capacity, col)
    received = lax.all_to_all(outgoing, DP, 0, 0, tiled=True)
    received = received.reshape(nx, ny, capacity, col).transpose(1, 2, 0, 3)
    received = received.reshape(ny * capacity, nx * col)
    received, third = lax.optimization_barrier((received, third))
    down[2], down[nz - 2] = third
    rows_in = lax.all_gather(received, MEM, axis=0)
    rows_in, mixed = lax.optimization_barrier((rows_in, mixed))
    rows_in = rows_in.reshape(nx, ny, ny * capacity, nx * col)
    gain = norm_gain.astype(f32).reshape(nx, ny, col).transpose(1, 0, 2).reshape(ny, 1, nx * col)
    hidden = hidden_of(
        rows_in,
        gain,
        gate_weight.reshape(nx, ny, col, ff),
        up_weight.reshape(nx, ny, col, ff),
        float(model_width),
    )

    half = hidden.shape[0] // 2
    blocks = {0: hidden}
    up_way, down_way = hidden, hidden
    for hops in range(1, nz // 2):
        up_way, down_way = along(up_way, 1), along(down_way, -1)
        blocks[hops], blocks[nz - hops] = up_way, down_way
    blocks[nz // 2] = jnp.concatenate([along(up_way[:half], 1), along(down_way[half:], -1)], axis=0)
    order = range(nz)
    kept, sent = down_project(core_at, [blocks[h] for h in order], [down[h] for h in order])
    expert_out = (kept + other_core(sent).astype(f32)).astype(bf16)
    expert_out = expert_out.reshape(rank_count, capacity, col)

    returned = lax.all_to_all(expert_out, DP, 0, 0, tiled=True)
    returned = returned.reshape(rank_count * capacity, col)
    slots = (routes * capacity + places).T
    matches = slots[:, :, None] == slot_index[None, None, :]
    combiner = jnp.sum(
        jnp.where(matches, route_weight.T[:, :, None], jnp.zeros((), route_weight.dtype)), axis=0
    )
    moe = jnp.dot(combiner, returned, preferred_element_type=f32)
    total = (mixed.T.astype(f32) + moe).astype(bf16)
    total = lax.all_to_all(total.reshape(members, tok_rows // members, col), MEM, 0, 0, tiled=True)
    return total.transpose(1, 0, 2).reshape(tok_rows // members, model_width)


def solution(mesh):
    dp, ep, tp = mesh.devices.shape
    nx = 1
    while nx * nx < dp:
        nx *= 2
    grid = Mesh(mesh.devices.reshape(nx, dp // nx, ep, tp), DP + MEM)
    in_specs = (
        P(DP, MEM, None),
        P(DP, None, None),
        P(DP, None, None),
        P(),
        P(),
        P(MEM, None, None),
        P(MEM, DP),
        P(DP, None),
        P(),
        P(DP, None),
        P(DP, None),
        P(DP, None, MEM),
        P(DP, None, MEM),
        P(DP, MEM, None),
    )
    out_specs = P(DP + MEM, None)
    return jax.shard_map(
        per_device, mesh=grid, in_specs=in_specs, out_specs=out_specs, check_vma=False
    )
```

```python
import functools

import jax
import jax.numpy as jnp
from jax import lax
from jax.experimental import pallas as pl
from jax.experimental.pallas import tpu as pltpu
from jax.sharding import PartitionSpec as P

score_scale = 192.0 ** (-0.5)
norm_eps = 1e-06
DP = ("dp",)
MEM = ("ep", "tp")
bf16 = jnp.bfloat16
f32 = jnp.float32
VMEM_LIMIT = 56 << 20
NN = (((1,), (0,)), ((), ()))
NT = (((1,), (1,)), ((), ()))


def params():
    return pltpu.CompilerParams(vmem_limit_bytes=VMEM_LIMIT)


def cost(flops, nbytes):
    return pl.CostEstimate(flops=flops, bytes_accessed=nbytes, transcendentals=0)


def attend_one(rows, length, prefix, prefix_dims, span, uv_ref, latent, store):
    total, span_rows = rows.shape[0], span.shape[0]
    keys_first = prefix_dims is NT
    cached = prefix[:, :latent] if keys_first else prefix[:latent]
    first = lax.dot_general(rows, prefix, prefix_dims, preferred_element_type=f32) * score_scale
    second = lax.dot_general(rows, span, NT, preferred_element_type=f32) * score_scale
    key = lax.broadcasted_iota(jnp.int32, first.shape, 1)
    first = jnp.where(key < length, first, -jnp.inf)
    token = lax.rem(lax.broadcasted_iota(jnp.int32, second.shape, 0), span_rows)
    late = lax.broadcasted_iota(jnp.int32, second.shape, 1)
    second = jnp.where(late <= token, second, -jnp.inf)
    highest = jnp.maximum(
        jnp.max(first, axis=1, keepdims=True), jnp.max(second, axis=1, keepdims=True)
    )
    first = jnp.exp(first - highest)
    second = jnp.exp(second - highest)
    norm = jnp.sum(first, axis=1, keepdims=True) + jnp.sum(second, axis=1, keepdims=True)
    first = (first / norm).astype(bf16)
    second = (second / norm).astype(bf16)
    out = lax.dot_general(first, cached, NN if keys_first else NT, preferred_element_type=f32)
    out += jnp.dot(second, span[:, :latent], preferred_element_type=f32)
    out = out.astype(bf16)
    for h in range(total // span_rows):
        part = jnp.dot(
            out[h * span_rows : (h + 1) * span_rows], uv_ref[h], preferred_element_type=f32
        )
        store(h, part.astype(bf16))


def own_kernel(rank_ref, lengths_ref, destination_ref, query_ref, prefix_ref, span_ref, uv_ref, out_ref, rows_ref):
    heads, latent, value = uv_ref.shape
    span_rows = span_ref.shape[1]
    here = prefix_ref.shape[0]
    turned = [query_ref[h].T for h in range(heads)]
    for j in range(here + rows_ref.shape[0]):
        at = slice(j * span_rows, (j + 1) * span_rows)
        rows = jnp.concatenate([turned[h][at] for h in range(heads)], axis=0)
        if j >= here:
            rows_ref[j - here] = rows
            continue

        def store(h, part):
            out_ref[at, h * value : (h + 1) * value] = part

        length = lengths_ref[rank_ref[0] * (here + rows_ref.shape[0]) + j]
        attend_one(rows, length, prefix_ref[j], NN, span_ref[j], uv_ref, latent, store)


def moved_kernel(rank_ref, lengths_ref, destination_ref, rows_ref, prefix_ref, span_ref, uv_ref, out_ref):
    heads, latent, value = uv_ref.shape
    here, _, width = rows_ref.shape
    span_rows = span_ref.shape[1]
    for j in range(here):
        at = slice(j * span_rows, (j + 1) * span_rows)

        def store(h, part):
            out_ref[at, h * value : (h + 1) * value] = part

        ranks = destination_ref.shape[1]
        requests = lengths_ref.shape[0] // ranks
        source = jnp.int32(0)
        for s in range(ranks):
            source = jnp.where(destination_ref[j, s] == rank_ref[0], jnp.int32(s), source)
        length = lengths_ref[source * requests + requests - here + j]
        prefix = prefix_ref[:, j].reshape(-1, width)
        attend_one(rows_ref[j], length, prefix, NT, span_ref[j], uv_ref, latent, store)


def attend_call(kernel, operands, specs, shapes):
    flops = 2 * 2 * 128 * (288 * (576 + 512) + 512 * 128)
    outs = [jax.ShapeDtypeStruct(shape, bf16) for shape in shapes]
    return pl.pallas_call(
        kernel,
        out_shape=outs,
        in_specs=[pl.BlockSpec(memory_space=pltpu.SMEM)] * 3 + specs,
        out_specs=[whole(shape) for shape in shapes],
        grid=(1,),
        compiler_params=params(),
        cost_estimate=cost(flops, 2 << 20),
    )(*operands)


def whole(shape, block=0):
    return pl.BlockSpec(tuple(shape), lambda i: (block,) + (0,) * (len(shape) - 1))


def share_kernel(values_ref, *refs):
    weight_refs, out_ref = refs[:-1], refs[-1]
    half = weight_refs[0].shape[1]
    each = out_ref.shape[1] // half
    for n, weight_ref in enumerate(weight_refs):
        product = lax.dot_general(
            weight_ref[0], values_ref[...], NT, preferred_element_type=f32
        ).astype(bf16)
        out_ref[n // each, (n % each) * half : (n % each + 1) * half] = product


def project(values, weights, layers):
    rows, depth = values.shape
    blocks, half, _ = weights.shape
    each = blocks // layers
    flight = 4
    weight_specs = [
        pl.BlockSpec((1, half, depth), lambda i, n=n: (flight * i + n, 0, 0)) for n in range(flight)
    ]
    return pl.pallas_call(
        share_kernel,
        out_shape=jax.ShapeDtypeStruct((layers, each * half, rows), bf16),
        grid=(blocks // flight,),
        in_specs=[pl.BlockSpec((rows, depth), lambda i: (0, 0))] + weight_specs,
        out_specs=pl.BlockSpec((flight // each, each * half, rows), lambda i: (i, 0, 0)),
        compiler_params=params(),
        cost_estimate=cost(
            2 * rows * depth * blocks * half,
            2 * (rows * depth + blocks * half * depth + blocks * half * rows),
        ),
    )(values, *([weights] * flight))


def hidden_kernel(width, core_ref, *refs):
    rows_refs, (gate_ref, up_ref, kept_ref, sent_ref, total, squares) = refs[:-6], refs[-6:]
    step = pl.program_id(0)
    weight = jnp.concatenate([gate_ref[...], up_ref[...]], axis=0)
    depth = rows_refs[0].shape[0]
    product, square = 0.0, 0.0
    for n, rows_ref in enumerate(rows_refs):
        block = rows_ref[...]
        piece = weight[:, n * depth : (n + 1) * depth]
        product += jnp.dot(piece, block, preferred_element_type=f32)
        widened = block.astype(f32)
        square += jnp.sum(widened * widened, axis=0, keepdims=True)

    @pl.when(step == 0)
    def _():
        total[...] = product
        squares[...] = square

    @pl.when(step > 0)
    def _():
        total[...] += product
        squares[...] += square

    @pl.when(step == pl.num_programs(0) - 1)
    def _():
        factor = lax.rsqrt(squares[...] / width + norm_eps)
        half, ff = kept_ref.shape
        gate = total[:ff] * factor
        up = total[ff:] * factor
        hidden = (gate / (1.0 + jnp.exp(-gate)) * up).T
        first = core_ref[0] == 0
        kept_ref[...] = jnp.where(first, hidden[:half], hidden[half:]).astype(bf16)
        sent_ref[...] = jnp.where(first, hidden[half:], hidden[:half]).astype(bf16)


def hidden_of(core, rows_in, weight_in):
    width, slots = rows_in.shape
    ff = weight_in.shape[0] // 2
    steps, flight = 4, 2
    depth = width // steps // flight
    rows_specs = [
        pl.BlockSpec((depth, slots), lambda i, n=n: (flight * i + n, 0)) for n in range(flight)
    ]
    return pl.pallas_call(
        functools.partial(hidden_kernel, float(width)),
        out_shape=[jax.ShapeDtypeStruct((slots // 2, ff), bf16)] * 2,
        grid=(steps,),
        in_specs=[
            pl.BlockSpec(memory_space=pltpu.SMEM),
            *rows_specs,
            pl.BlockSpec((ff, width // steps), lambda i: (0, i)),
            pl.BlockSpec((ff, width // steps), lambda i: (1, i)),
        ],
        out_specs=[pl.BlockSpec((slots // 2, ff), lambda i: (0, 0))] * 2,
        scratch_shapes=[pltpu.VMEM((2 * ff, slots), f32), pltpu.VMEM((1, slots), f32)],
        compiler_params=params(),
        cost_estimate=cost(4 * width * slots * ff, 2 * width * (slots + 2 * ff)),
    )(core, *([rows_in] * flight), weight_in, weight_in)


def dispatch_kernel(capacity, top_k, shares_ref, packed_ref, mixed_ref, out_ref):
    col = mixed_ref.shape[0]
    total = packed_ref[:col].astype(f32)
    total += jnp.sum(shares_ref[...].astype(f32), axis=0)
    mixed = total.astype(bf16)
    mixed_ref[...] = mixed
    notes = packed_ref[col:].astype(f32)
    slot = lax.broadcasted_iota(jnp.int32, (out_ref.shape[0], mixed.shape[1]), 0)
    hit = None
    for k in range(top_k):
        named = notes[k : k + 1] * capacity + notes[top_k + k : top_k + k + 1]
        same = slot == named.astype(jnp.int32)
        hit = same if hit is None else hit | same
    placer = jnp.where(hit, 1.0, 0.0).astype(bf16)
    out_ref[...] = lax.dot_general(placer, mixed, NT, preferred_element_type=f32).astype(bf16)


def dispatch(shares, packed, capacity, top_k, slots):
    col, rows = shares.shape[1:]
    return pl.pallas_call(
        functools.partial(dispatch_kernel, capacity, top_k),
        out_shape=[
            jax.ShapeDtypeStruct((col, rows), bf16),
            jax.ShapeDtypeStruct((slots, col), bf16),
        ],
        grid=(1,),
        in_specs=[whole(shares.shape), whole(packed.shape)],
        out_specs=[whole((col, rows)), whole((slots, col))],
        compiler_params=params(),
        cost_estimate=cost(2 * slots * col * rows, 2 * (9 * col * rows + slots * col)),
    )(shares, packed)


def slices_kernel(layer_ref, in_ref, *refs):
    count = len(refs) - 3
    outs, (held, in_sems, out_sems) = refs[:count], refs[count:]
    width = outs[0].shape[1]
    loads, stores = [], []
    for hops, out_ref in enumerate(outs):
        at = pl.multiple_of(lax.rem(layer_ref[0] + hops, count) * width, 128)
        loads.append(
            pltpu.make_async_copy(in_ref.at[:, pl.ds(at, width)], held.at[hops], in_sems.at[hops])
        )
        stores.append(pltpu.make_async_copy(held.at[hops], out_ref, out_sems.at[hops]))
    for load in loads:
        load.start()
    for load, store in zip(loads, stores):
        load.wait()
        store.start()
    for store in stores:
        store.wait()


def slices_of(layer, array, count):
    rows, columns = array.shape
    width = columns // count
    return pl.pallas_call(
        slices_kernel,
        out_shape=[jax.ShapeDtypeStruct((rows, width), array.dtype)] * count,
        in_specs=[
            pl.BlockSpec(memory_space=pltpu.SMEM),
            pl.BlockSpec(memory_space=pl.ANY),
        ],
        out_specs=[pl.BlockSpec(memory_space=pl.ANY)] * count,
        scratch_shapes=[
            pltpu.VMEM((count, rows, width), array.dtype),
            pltpu.SemaphoreType.DMA((count,)),
            pltpu.SemaphoreType.DMA((count,)),
        ],
        compiler_params=params(),
        cost_estimate=cost(0, 4 * rows * columns),
    )(layer, array)


def down_kernel(hidden_ref, *refs):
    weight_refs, (out_ref, total) = refs[:-2], refs[-2:]
    step = pl.program_id(0)
    weight = jnp.concatenate([ref[0, 0] for ref in weight_refs], axis=0)
    product = jnp.dot(hidden_ref[...], weight, preferred_element_type=f32)

    @pl.when(step == 0)
    def _():
        total[...] = product

    @pl.when(step > 0)
    def _():
        total[...] += product

    @pl.when(step == pl.num_programs(0) - 1)
    def _():
        out_ref[...] = total[...].astype(bf16)


def down_project(hidden, weights):
    rows = hidden.shape[0]
    hops, _, ff, cols = weights.shape
    steps = 4
    each = hops // steps
    return pl.pallas_call(
        down_kernel,
        out_shape=jax.ShapeDtypeStruct((rows, cols), bf16),
        grid=(steps,),
        in_specs=[
            pl.BlockSpec((rows, each * 2 * ff), lambda i: (0, i)),
            *[
                pl.BlockSpec((1, 1, ff, cols), lambda i, n=n: (each * i + n // 2, n % 2, 0, 0))
                for n in range(2 * each)
            ],
        ],
        out_specs=pl.BlockSpec((rows, cols), lambda i: (0, 0)),
        scratch_shapes=[pltpu.VMEM((rows, cols), f32)],
        compiler_params=params(),
        cost_estimate=cost(2 * rows * cols * hidden.shape[1], 5 << 20),
    )(hidden, *([weights] * (2 * each)))


def combine_kernel(group, core_ref, combiner_ref, rows_ref, mixed_ref, kept_ref, sent_ref):
    total = jnp.dot(combiner_ref[...], rows_ref[...], preferred_element_type=f32)
    first = core_ref[0] == 0
    half = mixed_ref.shape[0] // 2
    pieces = []
    for j in range(2):
        piece = mixed_ref[j * half : (j + 1) * half].astype(f32)
        nothing = jnp.zeros_like(piece)
        pieces += [jnp.where(first, piece, nothing), jnp.where(first, nothing, piece)]
    total += jnp.concatenate(pieces, axis=0).T
    total = total.reshape(-1, 2, group, total.shape[1])
    low, high = total[:, 0].reshape(kept_ref.shape), total[:, 1].reshape(kept_ref.shape)
    kept_ref[...] = jnp.where(first, low, high)
    sent_ref[...] = jnp.where(first, high, low).astype(bf16)


def combine(core, combiner, rows, mixed, group):
    shape = (combiner.shape[0] // 2, rows.shape[1])
    return pl.pallas_call(
        functools.partial(combine_kernel, group),
        out_shape=[jax.ShapeDtypeStruct(shape, f32), jax.ShapeDtypeStruct(shape, bf16)],
        grid=(1,),
        in_specs=[pl.BlockSpec(memory_space=pltpu.SMEM)]
        + [whole(o.shape) for o in (combiner, rows, mixed)],
        out_specs=[whole(shape)] * 2,
        compiler_params=params(),
        cost_estimate=cost(4 * shape[0] * shape[1] * rows.shape[0], 1 << 20),
    )(core, combiner, rows, mixed)


def places_of(route_rows, experts):
    flat_routes = route_rows.reshape(-1)
    hits = (flat_routes[:, None] == jnp.arange(experts, dtype=jnp.int32)[None, :]).astype(jnp.int32)
    earlier = jnp.cumsum(hits, axis=0) - hits
    return jnp.sum(earlier * hits, axis=1).reshape(route_rows.shape)


def per_device(
    queries,
    cache,
    span_latent,
    prefix_len,
    destination,
    uv_weight,
    out_weight,
    residual,
    norm_gain,
    routes,
    route_weight,
    gate_weight,
    up_weight,
    down_weight,
):
    requests, prefix_rows, cached_width = cache.shape
    tok_rows = queries.shape[0]
    model_width = residual.shape[1]
    top_k = routes.shape[1]
    ff = gate_weight.shape[2]
    nz = lax.axis_size("ep")
    rank_count = lax.axis_size(DP)
    members = lax.axis_size(MEM)
    my_rank = lax.axis_index(DP)
    member = lax.axis_index(MEM)
    layer = lax.axis_index("ep")
    core = lax.axis_index("tp")
    core_at = jnp.reshape(core, (1,))
    col = model_width // members
    capacity = max(2, 3 * tok_rows * top_k // (2 * rank_count))

    def other_core(array):
        return lax.ppermute(array, "tp", [(0, 1), (1, 0)])

    def along(array, hops):
        return lax.ppermute(array, "ep", [(z, (z + hops) % nz) for z in range(nz)])

    ranks = jnp.arange(rank_count, dtype=jnp.int32)
    source_first = jnp.sum(ranks * (destination[0] == my_rank).astype(jnp.int32))
    source_second = jnp.sum(ranks * (destination[1] == my_rank).astype(jnp.int32))
    part = prefix_rows // members
    moving = lax.dynamic_slice_in_dim(cache[requests - 2 :], member * part, part, 1)
    arrived = lax.all_to_all(
        jnp.broadcast_to(moving[None], (rank_count,) + moving.shape), DP, 0, 0, tiled=True
    )
    turned_out = out_weight.T.reshape(2, col // 2, -1)
    out_mine = lax.dynamic_index_in_dim(turned_out, core, 0, keepdims=False)
    out_other = other_core(lax.dynamic_index_in_dim(turned_out, 1 - core, 0, keepdims=False))
    out_cols = lax.all_gather(jnp.concatenate([out_mine, out_other], axis=1), DP, axis=0)
    slices = slices_of(jnp.reshape(layer, (1,)), down_weight[0], nz)
    middle = nz // 2
    half_ff = ff // 2

    down = {0: slices[0], 1: along(slices[1], 1), nz - 1: along(slices[nz - 1], -1)}
    arrived, down = lax.optimization_barrier((arrived, down))
    chosen = jnp.stack(
        [
            lax.dynamic_index_in_dim(arrived[:, 0], source_first, 0, keepdims=False),
            lax.dynamic_index_in_dim(arrived[:, 1], source_second, 0, keepdims=False),
        ]
    )
    moved = lax.all_gather(chosen, MEM, axis=0)

    window, held = lax.optimization_barrier(
        ((slices[3], slices[nz - 3], slices[middle]), (cache, routes, norm_gain, moved))
    )
    cache, routes, norm_gain, moved = held
    window = (
        along(window[0], 3),
        along(window[1], -3),
        along(window[2][:half_ff], middle),
        along(window[2][half_ff:], -middle),
    )

    heads, latent = queries.shape[1], uv_weight.shape[1]
    value = uv_weight.shape[2]
    here = requests - 2
    span_rows = span_latent.shape[1]
    values_shape = (2 * span_rows, heads * value)
    turned = (queries.transpose(1, 2, 0), cache.transpose(0, 2, 1))
    spans = (2, span_rows, cached_width)
    scalars = (jnp.reshape(my_rank, (1,)).astype(jnp.int32), prefix_len, destination)
    values_own, query_rows = attend_call(
        own_kernel,
        (*scalars, *turned, span_latent, uv_weight),
        [
            whole(turned[0].shape),
            whole((here, cached_width, prefix_rows)),
            whole(spans),
            whole(uv_weight.shape),
        ],
        [values_shape, (2, heads * span_rows, cached_width)],
    )

    (values_moved,) = attend_call(
        moved_kernel,
        (*scalars, query_rows, moved, span_latent, uv_weight),
        [whole(query_rows.shape), whole(moved.shape), whole(spans, 1), whole(uv_weight.shape)],
        [values_shape],
    )
    values = jnp.concatenate([values_own, values_moved], axis=0)

    places = places_of(routes, rank_count)
    residual_t = lax.dynamic_slice_in_dim(residual, layer * 2 * col, 2 * col, 1).T
    residual_t = residual_t.reshape(2, 2, col // 2, tok_rows)
    residual_t = lax.dynamic_index_in_dim(residual_t, core, 1, keepdims=False)
    packed = jnp.concatenate(
        [
            residual_t.reshape(col, tok_rows),
            routes.T.astype(bf16),
            places.T.astype(bf16),
            jnp.zeros((16 - 2 * top_k, tok_rows), bf16),
        ],
        axis=0,
    )
    halves = jnp.arange(capacity // 2, dtype=jnp.int32) + core * (capacity // 2)
    slot_index = jnp.arange(rank_count, dtype=jnp.int32)[:, None] * capacity + halves[None, :]
    slots = (routes * capacity + places).T
    matches = slots[:, :, None] == slot_index.reshape(-1)[None, None, :]
    combiner = jnp.sum(
        jnp.where(matches, route_weight.T[:, :, None], jnp.zeros((), route_weight.dtype)), axis=0
    )
    gain = norm_gain.astype(f32)[:, None]
    weight_in = jnp.concatenate([gate_weight[0], up_weight[0]], axis=1)
    weight_in = (weight_in.astype(f32) * gain).astype(bf16)
    weight_in = weight_in.reshape(nz, 2, 2, col // 2, 2 * ff).transpose(0, 2, 1, 3, 4)
    weight_in = weight_in.reshape(model_width, 2 * ff).T

    values = jnp.concatenate([values, other_core(values)], axis=1)
    out_cols, window, packed, combiner, weight_in = lax.optimization_barrier(
        (out_cols, window, packed, combiner, weight_in)
    )
    down[3], down[nz - 3] = window[:2]
    down[middle] = jnp.concatenate(window[2:], axis=0)
    shares = project(values, out_cols, nz)
    shares = lax.all_to_all(shares, "ep", 0, 0, tiled=True)
    shares, down = lax.optimization_barrier((shares, down))

    window, _ = lax.optimization_barrier(((slices[2], slices[nz - 2]), shares))
    window = (along(window[0], 2), along(window[1], -2))
    mixed, outgoing = dispatch(shares, packed, capacity, top_k, rank_count * capacity)
    outgoing = outgoing.reshape(rank_count, capacity, col)
    received = lax.all_to_all(outgoing, DP, 0, 0, tiled=True)
    received, window = lax.optimization_barrier((received, window))
    down[2], down[nz - 2] = window
    received = received.reshape(rank_count, 2, capacity // 2, col).transpose(3, 1, 0, 2)
    received = received.reshape(col, rank_count * capacity)
    down, _ = lax.optimization_barrier((down, received))
    down_mine = jnp.stack([down[h] for h in range(nz)])
    down_all = jnp.stack([down_mine, other_core(down_mine)], axis=1)
    rows_in = lax.all_gather(received, MEM, axis=0)
    rows_in, down_all = lax.optimization_barrier((rows_in, down_all))
    hidden, sent = hidden_of(core_at, rows_in.reshape(model_width, -1), weight_in)

    hidden = jnp.concatenate([hidden, other_core(sent)], axis=1)
    half = hidden.shape[0] // 2
    blocks = {0: hidden}
    up_way, down_way = hidden, hidden
    for hops in range(1, middle):
        up_way, down_way = along(up_way, 1), along(down_way, -1)
        blocks[hops], blocks[nz - hops] = up_way, down_way
    blocks[middle] = jnp.concatenate([along(up_way[:half], 1), along(down_way[half:], -1)], axis=0)
    hidden_all = jnp.concatenate([blocks[h] for h in range(nz)], axis=1)
    expert_out = down_project(hidden_all, down_all)
    expert_out = expert_out.reshape(rank_count, capacity // 2, 2 * col)

    returned = lax.all_to_all(expert_out, DP, 0, 0, tiled=True)
    returned = returned.reshape(rank_count * capacity // 2, 2 * col)
    group = tok_rows // members
    kept, sent = combine(core_at, combiner, returned, mixed, group)
    total = (kept + other_core(sent).astype(f32)).astype(bf16)
    total = lax.all_to_all(total.reshape(nz, group, 2 * col), "ep", 0, 0, tiled=True)
    return total.transpose(1, 0, 2).reshape(group, model_width)


def solution(mesh):
    in_specs = (
        P(DP, MEM, None),
        P(DP, None, None),
        P(DP, None, None),
        P(),
        P(),
        P(MEM, None, None),
        P(MEM, DP),
        P(DP, None),
        P(),
        P(DP, None),
        P(DP, None),
        P(DP, None, MEM),
        P(DP, None, MEM),
        P(DP, MEM, None),
    )
    out_specs = P(DP + MEM, None)
    return jax.shard_map(
        per_device, mesh=mesh, in_specs=in_specs, out_specs=out_specs, check_vma=False
    )
```

```python
import functools

import jax
import jax.numpy as jnp
from jax import lax
from jax.experimental import pallas as pl
from jax.experimental.pallas import tpu as pltpu
from jax.sharding import PartitionSpec as P

score_scale = 192.0 ** (-0.5)
norm_eps = 1e-06
DP = ("dp",)
MEM = ("ep", "tp")
bf16 = jnp.bfloat16
f32 = jnp.float32
VMEM_LIMIT = 56 << 20
NN = (((1,), (0,)), ((), ()))
NT = (((1,), (1,)), ((), ()))


def params():
    return pltpu.CompilerParams(vmem_limit_bytes=VMEM_LIMIT)


def cost(flops, nbytes):
    return pl.CostEstimate(flops=flops, bytes_accessed=nbytes, transcendentals=0)


def attend_one(rows, length, prefix, prefix_dims, span, uv_ref, latent, store, place=None):
    total, span_rows = rows.shape[0], span.shape[0]
    keys_first = prefix_dims is NT
    cached = prefix[:, :latent] if keys_first else prefix[:latent]
    first = lax.dot_general(rows, prefix, prefix_dims, preferred_element_type=f32) * score_scale
    second = lax.dot_general(rows, span, NT, preferred_element_type=f32) * score_scale
    key = lax.broadcasted_iota(jnp.int32, first.shape, 1)
    if place is not None:
        key = place(key)
    first = jnp.where(key < length, first, -jnp.inf)
    token = lax.rem(lax.broadcasted_iota(jnp.int32, second.shape, 0), span_rows)
    late = lax.broadcasted_iota(jnp.int32, second.shape, 1)
    second = jnp.where(late <= token, second, -jnp.inf)
    highest = jnp.maximum(
        jnp.max(first, axis=1, keepdims=True), jnp.max(second, axis=1, keepdims=True)
    )
    first = jnp.exp(first - highest)
    second = jnp.exp(second - highest)
    norm = jnp.sum(first, axis=1, keepdims=True) + jnp.sum(second, axis=1, keepdims=True)
    first = (first / norm).astype(bf16)
    second = (second / norm).astype(bf16)
    out = lax.dot_general(first, cached, NN if keys_first else NT, preferred_element_type=f32)
    out += jnp.dot(second, span[:, :latent], preferred_element_type=f32)
    out = out.astype(bf16)
    for h in range(total // span_rows):
        part = jnp.dot(
            out[h * span_rows : (h + 1) * span_rows], uv_ref[h], preferred_element_type=f32
        )
        store(h, part.astype(bf16))


def own_kernel(rank_ref, lengths_ref, destination_ref, query_ref, prefix_ref, span_ref, uv_ref, out_ref, rows_ref):
    heads, latent, value = uv_ref.shape
    span_rows = span_ref.shape[1]
    here = prefix_ref.shape[0]
    turned = [query_ref[h].T for h in range(heads)]
    for j in range(here + rows_ref.shape[0]):
        at = slice(j * span_rows, (j + 1) * span_rows)
        rows = jnp.concatenate([turned[h][at] for h in range(heads)], axis=0)
        if j >= here:
            rows_ref[j - here] = rows
            continue

        def store(h, part):
            out_ref[at, h * value : (h + 1) * value] = part

        length = lengths_ref[rank_ref[0] * (here + rows_ref.shape[0]) + j]
        attend_one(rows, length, prefix_ref[j], NN, span_ref[j], uv_ref, latent, store)


def moved_kernel(
    rank_ref,
    lengths_ref,
    destination_ref,
    member_ref,
    rows_ref,
    mine_ref,
    other_ref,
    span_ref,
    uv_ref,
    out_ref,
):
    heads, latent, value = uv_ref.shape
    here, _, width = rows_ref.shape
    span_rows = span_ref.shape[1]
    hops, _, part, _ = mine_ref.shape

    def place(key):
        side = lax.div(key, hops * part)
        hop = lax.rem(lax.div(key, part), hops)
        layer = lax.rem(member_ref[0] - hop + hops, hops)
        core = jnp.where(side == 0, member_ref[1], 1 - member_ref[1])
        return (layer * 2 + core) * part + lax.rem(key, part)

    for j in range(here):
        at = slice(j * span_rows, (j + 1) * span_rows)

        def store(h, part):
            out_ref[at, h * value : (h + 1) * value] = part

        ranks = destination_ref.shape[1]
        requests = lengths_ref.shape[0] // ranks
        source = jnp.int32(0)
        for s in range(ranks):
            source = jnp.where(destination_ref[j, s] == rank_ref[0], jnp.int32(s), source)
        length = lengths_ref[source * requests + requests - here + j]
        prefix = jnp.concatenate(
            [mine_ref[:, j].reshape(-1, width), other_ref[:, j].reshape(-1, width)], axis=0
        )
        attend_one(
            rows_ref[j], length, prefix, NT, span_ref[j], uv_ref, latent, store, place
        )


def attend_call(kernel, operands, specs, shapes):
    flops = 2 * 2 * 128 * (288 * (576 + 512) + 512 * 128)
    outs = [jax.ShapeDtypeStruct(shape, bf16) for shape in shapes]
    return pl.pallas_call(
        kernel,
        out_shape=outs,
        in_specs=[pl.BlockSpec(memory_space=pltpu.SMEM)] * (len(operands) - len(specs)) + specs,
        out_specs=[whole(shape) for shape in shapes],
        grid=(1,),
        compiler_params=params(),
        cost_estimate=cost(flops, 2 << 20),
    )(*operands)


def whole(shape, block=0):
    return pl.BlockSpec(tuple(shape), lambda i: (block,) + (0,) * (len(shape) - 1))


def share_kernel(values_ref, weight_ref, out_ref, turned):
    @pl.when(pl.program_id(0) == 0)
    def _():
        turned[...] = values_ref[...].T

    blocks, half, depth = weight_ref.shape
    weight = weight_ref[...].reshape(blocks * half, depth)
    product = jnp.dot(weight, turned[...], preferred_element_type=f32).astype(bf16)
    out_ref[...] = product.reshape(out_ref.shape)


def project(values, weights, layers):
    rows, depth = values.shape
    blocks, half, _ = weights.shape
    each = blocks // layers
    steps = 2
    return pl.pallas_call(
        share_kernel,
        out_shape=jax.ShapeDtypeStruct((layers, each * half, rows), bf16),
        grid=(steps,),
        in_specs=[
            pl.BlockSpec((rows, depth), lambda i: (0, 0)),
            pl.BlockSpec((blocks // steps, half, depth), lambda i: (i, 0, 0)),
        ],
        out_specs=pl.BlockSpec((layers // steps, each * half, rows), lambda i: (i, 0, 0)),
        scratch_shapes=[pltpu.VMEM((depth, rows), bf16)],
        compiler_params=params(),
        cost_estimate=cost(
            2 * rows * depth * blocks * half,
            2 * (rows * depth + blocks * half * depth + blocks * half * rows),
        ),
    )(values, weights)


def hidden_kernel(width, rows_ref, weight_ref, out_ref, total, squares):
    step = pl.program_id(0)
    block = rows_ref[...]
    product = jnp.dot(weight_ref[...], block, preferred_element_type=f32)
    widened = block.astype(f32)
    square = jnp.sum(widened * widened, axis=0, keepdims=True)

    @pl.when(step == 0)
    def _():
        total[...] = product
        squares[...] = square

    @pl.when(step > 0)
    def _():
        total[...] += product
        squares[...] += square

    @pl.when(step == pl.num_programs(0) - 1)
    def _():
        factor = lax.rsqrt(squares[...] / width + norm_eps)
        ff = out_ref.shape[1]
        gate = total[:ff] * factor
        up = total[ff:] * factor
        out_ref[...] = (gate / (1.0 + jnp.exp(-gate)) * up).T.astype(bf16)


def hidden_of(rows_in, weight_in):
    width, slots = rows_in.shape
    ff = weight_in.shape[0] // 2
    steps = 2
    return pl.pallas_call(
        functools.partial(hidden_kernel, float(width)),
        out_shape=jax.ShapeDtypeStruct((slots, ff), bf16),
        grid=(steps,),
        in_specs=[
            pl.BlockSpec((width // steps, slots), lambda i: (i, 0)),
            pl.BlockSpec((2 * ff, width // steps), lambda i: (0, i)),
        ],
        out_specs=pl.BlockSpec((slots, ff), lambda i: (0, 0)),
        scratch_shapes=[pltpu.VMEM((2 * ff, slots), f32), pltpu.VMEM((1, slots), f32)],
        compiler_params=params(),
        cost_estimate=cost(4 * width * slots * ff, 2 * width * (slots + 2 * ff)),
    )(rows_in, weight_in)


def dispatch_kernel(capacity, top_k, shares_ref, packed_ref, mixed_ref, out_ref):
    col = mixed_ref.shape[0]
    total = packed_ref[:col].astype(f32)
    total += jnp.sum(shares_ref[...].astype(f32), axis=0)
    mixed = total.astype(bf16)
    mixed_ref[...] = mixed
    notes = packed_ref[col:].astype(f32)
    slot = lax.broadcasted_iota(jnp.int32, (out_ref.shape[0], mixed.shape[1]), 0)
    hit = None
    for k in range(top_k):
        named = notes[k : k + 1] * capacity + notes[top_k + k : top_k + k + 1]
        same = slot == named.astype(jnp.int32)
        hit = same if hit is None else hit | same
    placer = jnp.where(hit, 1.0, 0.0).astype(bf16)
    out_ref[...] = lax.dot_general(placer, mixed, NT, preferred_element_type=f32).astype(bf16)


def dispatch(shares, packed, capacity, top_k, slots):
    col, rows = shares.shape[1:]
    return pl.pallas_call(
        functools.partial(dispatch_kernel, capacity, top_k),
        out_shape=[
            jax.ShapeDtypeStruct((col, rows), bf16),
            jax.ShapeDtypeStruct((slots, col), bf16),
        ],
        grid=(1,),
        in_specs=[whole(shares.shape), whole(packed.shape)],
        out_specs=[whole((col, rows)), whole((slots, col))],
        compiler_params=params(),
        cost_estimate=cost(2 * slots * col * rows, 2 * (9 * col * rows + slots * col)),
    )(shares, packed)


def slices_kernel(layer_ref, in_ref, *refs):
    outs, (held, in_sems, out_sems) = refs[:-3], refs[-3:]
    count, rows, width = held.shape
    loads, stores = [], []
    for hops in range(count):
        at = pl.multiple_of(lax.rem(layer_ref[0] + hops, count) * width, 128)
        loads.append(
            pltpu.make_async_copy(in_ref.at[:, pl.ds(at, width)], held.at[hops], in_sems.at[hops])
        )
        stores.append(pltpu.make_async_copy(held.at[hops], outs[hops], out_sems.at[hops]))
    half = rows // 2
    stores[count // 2] = pltpu.make_async_copy(
        held.at[count // 2, pl.ds(0, half)], outs[count // 2], out_sems.at[count // 2]
    )
    stores.append(
        pltpu.make_async_copy(
            held.at[count // 2, pl.ds(half, half)], outs[count], out_sems.at[count]
        )
    )
    for load in loads:
        load.start()
    for hops, load in enumerate(loads):
        load.wait()
        stores[hops].start()
        if hops == count // 2:
            stores[count].start()
    for store in stores:
        store.wait()


def slices_of(layer, array, count):
    rows, columns = array.shape
    width = columns // count
    shapes = [(rows, width)] * (count + 1)
    shapes[count // 2] = shapes[count] = (rows // 2, width)
    return pl.pallas_call(
        slices_kernel,
        out_shape=[jax.ShapeDtypeStruct(shape, array.dtype) for shape in shapes],
        in_specs=[
            pl.BlockSpec(memory_space=pltpu.SMEM),
            pl.BlockSpec(memory_space=pl.ANY),
        ],
        out_specs=[pl.BlockSpec(memory_space=pl.ANY)] * (count + 1),
        scratch_shapes=[
            pltpu.VMEM((count, rows, width), array.dtype),
            pltpu.SemaphoreType.DMA((count,)),
            pltpu.SemaphoreType.DMA((count + 1,)),
        ],
        compiler_params=params(),
        cost_estimate=cost(0, 4 * rows * columns),
    )(layer, array)


def down_kernel(mine_ref, other_ref, mine_weight_ref, other_weight_ref, out_ref):
    depth = mine_ref.shape[1]
    total = jnp.dot(
        mine_ref[...], mine_weight_ref[...].reshape(depth, -1), preferred_element_type=f32
    )
    total += jnp.dot(
        other_ref[...], other_weight_ref[...].reshape(depth, -1), preferred_element_type=f32
    )
    out_ref[...] = total.astype(bf16)


def down_project(*operands):
    shape = (operands[0].shape[0], operands[2].shape[2])
    return pl.pallas_call(
        down_kernel,
        out_shape=jax.ShapeDtypeStruct(shape, bf16),
        grid=(1,),
        in_specs=[whole(o.shape) for o in operands],
        out_specs=whole(shape),
        compiler_params=params(),
        cost_estimate=cost(4 * shape[0] * shape[1] * operands[0].shape[1], 5 << 20),
    )(*operands)


def combine_kernel(combiner_ref, rows_ref, mixed_ref, out_ref):
    total = jnp.dot(combiner_ref[...], rows_ref[...], preferred_element_type=f32)
    out_ref[...] = (total + mixed_ref[...].astype(f32).T).astype(bf16)


def combine(combiner, rows, mixed):
    shape = (combiner.shape[0], rows.shape[1])
    return pl.pallas_call(
        combine_kernel,
        out_shape=jax.ShapeDtypeStruct(shape, bf16),
        grid=(1,),
        in_specs=[whole(o.shape) for o in (combiner, rows, mixed)],
        out_specs=whole(shape),
        compiler_params=params(),
        cost_estimate=cost(2 * shape[0] * shape[1] * rows.shape[0], 1 << 20),
    )(combiner, rows, mixed)


def places_of(route_rows, experts):
    flat_routes = route_rows.reshape(-1)
    hits = (flat_routes[:, None] == jnp.arange(experts, dtype=jnp.int32)[None, :]).astype(jnp.int32)
    earlier = jnp.cumsum(hits, axis=0) - hits
    return jnp.sum(earlier * hits, axis=1).reshape(route_rows.shape)


def per_device(
    queries,
    cache,
    span_latent,
    prefix_len,
    destination,
    uv_weight,
    out_weight,
    residual,
    norm_gain,
    routes,
    route_weight,
    gate_weight,
    up_weight,
    down_weight,
):
    requests, prefix_rows, cached_width = cache.shape
    tok_rows = queries.shape[0]
    model_width = residual.shape[1]
    top_k = routes.shape[1]
    ff = gate_weight.shape[2]
    nz = lax.axis_size("ep")
    rank_count = lax.axis_size(DP)
    members = lax.axis_size(MEM)
    my_rank = lax.axis_index(DP)
    member = lax.axis_index(MEM)
    layer = lax.axis_index("ep")
    core = lax.axis_index("tp")
    col = model_width // members
    capacity = max(2, 3 * tok_rows * top_k // (2 * rank_count))

    def other_core(array):
        return lax.ppermute(array, "tp", [(0, 1), (1, 0)])

    def along(array, hops):
        return lax.ppermute(array, "ep", [(z, (z + hops) % nz) for z in range(nz)])

    ranks = jnp.arange(rank_count, dtype=jnp.int32)
    source_first = jnp.sum(ranks * (destination[0] == my_rank).astype(jnp.int32))
    source_second = jnp.sum(ranks * (destination[1] == my_rank).astype(jnp.int32))
    part = prefix_rows // members
    moving = lax.dynamic_slice_in_dim(cache[requests - 2 :], member * part, part, 1)
    arrived = lax.all_to_all(
        jnp.broadcast_to(moving[None], (rank_count,) + moving.shape), DP, 0, 0, tiled=True
    )
    turned_out = out_weight.T.reshape(2, col // 2, -1)
    out_mine = lax.dynamic_index_in_dim(turned_out, core, 0, keepdims=False)
    out_other = other_core(lax.dynamic_index_in_dim(turned_out, 1 - core, 0, keepdims=False))
    out_cols = lax.all_gather(jnp.concatenate([out_mine, out_other], axis=1), DP, axis=0)
    slices = slices_of(jnp.reshape(layer, (1,)), down_weight[0], nz)
    middle = nz // 2

    down = {0: slices[0], 1: along(slices[1], 1), nz - 1: along(slices[nz - 1], -1)}
    arrived, down = lax.optimization_barrier((arrived, down))
    chosen = jnp.stack(
        [
            lax.dynamic_index_in_dim(arrived[:, 0], source_first, 0, keepdims=False),
            lax.dynamic_index_in_dim(arrived[:, 1], source_second, 0, keepdims=False),
        ]
    )
    moved = [chosen] + [along(chosen, hops) for hops in range(1, nz)]
    first_piece = moved[1]
    moved = jnp.stack(moved)

    window, cache, routes, _ = lax.optimization_barrier((slices[2:], cache, routes, first_piece))
    window = {hops: piece for hops, piece in enumerate(window, 2)}
    window = [
        along(window[middle], middle),
        along(window[nz], -middle),
        along(window[3], 3),
        along(window[nz - 3], -3),
        along(window[2], 2),
        along(window[nz - 2], -2),
    ]

    heads, latent = queries.shape[1], uv_weight.shape[1]
    value = uv_weight.shape[2]
    here = requests - 2
    span_rows = span_latent.shape[1]
    values_shape = (2 * span_rows, heads * value)
    turned = (queries.transpose(1, 2, 0), cache.transpose(0, 2, 1))
    spans = (2, span_rows, cached_width)
    scalars = (jnp.reshape(my_rank, (1,)).astype(jnp.int32), prefix_len, destination)
    values_own, query_rows = attend_call(
        own_kernel,
        (*scalars, *turned, span_latent, uv_weight),
        [
            whole(turned[0].shape),
            whole((here, cached_width, prefix_rows)),
            whole(spans),
            whole(uv_weight.shape),
        ],
        [values_shape, (2, heads * span_rows, cached_width)],
    )

    member_at = jnp.stack([layer, core]).astype(jnp.int32)
    moved_other = other_core(moved)
    (values_moved,) = attend_call(
        moved_kernel,
        (*scalars, member_at, query_rows, moved, moved_other, span_latent, uv_weight),
        [
            whole(query_rows.shape),
            whole(moved.shape),
            whole(moved.shape),
            whole(spans, 1),
            whole(uv_weight.shape),
        ],
        [values_shape],
    )
    values = jnp.concatenate([values_own, values_moved], axis=0)

    places = places_of(routes, rank_count)
    residual_t = lax.dynamic_slice_in_dim(residual, layer * 2 * col, 2 * col, 1).T
    residual_t = residual_t.reshape(2, 2, col // 2, tok_rows)
    residual_t = lax.dynamic_index_in_dim(residual_t, core, 1, keepdims=False)
    packed = jnp.concatenate(
        [
            residual_t.reshape(col, tok_rows),
            routes.T.astype(bf16),
            places.T.astype(bf16),
            jnp.zeros((16 - 2 * top_k, tok_rows), bf16),
        ],
        axis=0,
    )
    values = jnp.concatenate([values, other_core(values)], axis=1)
    out_cols, window, packed = lax.optimization_barrier((out_cols, window, packed))
    down[middle] = jnp.concatenate(window[:2], axis=0)
    down[3], down[nz - 3] = window[2:4]
    down[2], down[nz - 2] = window[4:]
    shares = project(values, out_cols, nz)

    norm_gain, route_weight, shares = lax.optimization_barrier((norm_gain, route_weight, shares))
    slot_index = jnp.arange(rank_count * capacity, dtype=jnp.int32)
    slots = (routes * capacity + places).T
    matches = slots[:, :, None] == slot_index[None, None, :]
    combiner = jnp.sum(
        jnp.where(matches, route_weight.T[:, :, None], jnp.zeros((), route_weight.dtype)), axis=0
    )
    gain = norm_gain.astype(f32)[:, None]
    weight_in = jnp.concatenate([gate_weight[0], up_weight[0]], axis=1)
    weight_in = (weight_in.astype(f32) * gain).astype(bf16)
    weight_in = weight_in.reshape(nz, 2, 2, col // 2, 2 * ff).transpose(0, 2, 1, 3, 4)
    weight_in = weight_in.reshape(model_width, 2 * ff).T
    shares = lax.all_to_all(shares, "ep", 0, 0, tiled=True)
    shares, down, combiner, weight_in = lax.optimization_barrier(
        (shares, down, combiner, weight_in)
    )

    mixed, outgoing = dispatch(shares, packed, capacity, top_k, rank_count * capacity)
    outgoing = outgoing.reshape(rank_count, capacity, col)
    received = lax.all_to_all(outgoing, DP, 0, 0, tiled=True)
    received = received.reshape(rank_count * capacity, col).T
    down, _ = lax.optimization_barrier((down, received))
    down_all = jnp.stack([down[h] for h in range(nz)])
    half = col // 2
    even = jnp.concatenate([down_all[..., :half], down_all[..., col : col + half]], axis=2)
    odd = jnp.concatenate([down_all[..., half:col], down_all[..., col + half :]], axis=2)
    down_mine = jnp.where(core == 0, even, odd)
    down_other = other_core(jnp.where(core == 0, odd, even))
    rows_in = lax.all_gather(received, MEM, axis=0)
    rows_in, down_mine, down_other = lax.optimization_barrier((rows_in, down_mine, down_other))
    hidden = hidden_of(rows_in.reshape(model_width, -1), weight_in)

    half = hidden.shape[0] // 2
    blocks = {0: hidden}
    up_way, down_way = hidden, hidden
    for hops in range(1, middle):
        up_way, down_way = along(up_way, 1), along(down_way, -1)
        blocks[hops], blocks[nz - hops] = up_way, down_way
    blocks[middle] = jnp.concatenate([along(up_way[:half], 1), along(down_way[half:], -1)], axis=0)
    hidden_all = jnp.concatenate([blocks[h] for h in range(nz)], axis=1)
    expert_out = down_project(hidden_all, other_core(hidden_all), down_mine, down_other)
    expert_out = expert_out.reshape(rank_count, capacity, col)

    returned = lax.all_to_all(expert_out, DP, 0, 0, tiled=True)
    total = combine(combiner, returned.reshape(rank_count * capacity, col), mixed)
    group = tok_rows // members
    total = lax.all_to_all(total.reshape(members, group, col), MEM, 0, 0, tiled=True)
    total = total.reshape(nz, 2, group, 2, col // 2).transpose(2, 0, 3, 1, 4)
    return total.reshape(group, model_width)


def solution(mesh):
    in_specs = (
        P(DP, MEM, None),
        P(DP, None, None),
        P(DP, None, None),
        P(),
        P(),
        P(MEM, None, None),
        P(MEM, DP),
        P(DP, None),
        P(),
        P(DP, None),
        P(DP, None),
        P(DP, None, MEM),
        P(DP, None, MEM),
        P(DP, MEM, None),
    )
    out_specs = P(DP + MEM, None)
    return jax.shard_map(
        per_device, mesh=mesh, in_specs=in_specs, out_specs=out_specs, check_vma=False
    )
```

```python
import functools

import jax
import jax.numpy as jnp
from jax import lax
from jax.experimental import pallas as pl
from jax.experimental.pallas import tpu as pltpu
from jax.sharding import PartitionSpec as P

score_scale = 192.0 ** (-0.5)
norm_eps = 1e-06
DP = ("dp",)
MEM = ("ep", "tp")
bf16 = jnp.bfloat16
f32 = jnp.float32
VMEM_LIMIT = 56 << 20
NN = (((1,), (0,)), ((), ()))
NT = (((1,), (1,)), ((), ()))


def params():
    return pltpu.CompilerParams(vmem_limit_bytes=VMEM_LIMIT)


def cost(flops, nbytes):
    return pl.CostEstimate(flops=flops, bytes_accessed=nbytes, transcendentals=0)


def attend_one(rows, length, prefix, prefix_dims, span, uv_ref, latent, store):
    total, span_rows = rows.shape[0], span.shape[0]
    keys_first = prefix_dims is NT
    cached = prefix[:, :latent] if keys_first else prefix[:latent]
    first = lax.dot_general(rows, prefix, prefix_dims, preferred_element_type=f32) * score_scale
    second = lax.dot_general(rows, span, NT, preferred_element_type=f32) * score_scale
    key = lax.broadcasted_iota(jnp.int32, first.shape, 1)
    first = jnp.where(key < length, first, -jnp.inf)
    token = lax.rem(lax.broadcasted_iota(jnp.int32, second.shape, 0), span_rows)
    late = lax.broadcasted_iota(jnp.int32, second.shape, 1)
    second = jnp.where(late <= token, second, -jnp.inf)
    highest = jnp.maximum(
        jnp.max(first, axis=1, keepdims=True), jnp.max(second, axis=1, keepdims=True)
    )
    first = jnp.exp(first - highest)
    second = jnp.exp(second - highest)
    norm = jnp.sum(first, axis=1, keepdims=True) + jnp.sum(second, axis=1, keepdims=True)
    first = (first / norm).astype(bf16)
    second = (second / norm).astype(bf16)
    out = lax.dot_general(first, cached, NN if keys_first else NT, preferred_element_type=f32)
    out += jnp.dot(second, span[:, :latent], preferred_element_type=f32)
    out = out.astype(bf16)
    for h in range(total // span_rows):
        part = jnp.dot(
            out[h * span_rows : (h + 1) * span_rows], uv_ref[h], preferred_element_type=f32
        )
        store(h, part.astype(bf16))


def own_kernel(rank_ref, lengths_ref, destination_ref, query_ref, prefix_ref, span_ref, uv_ref, out_ref, rows_ref):
    heads, latent, value = uv_ref.shape
    span_rows = span_ref.shape[1]
    here = prefix_ref.shape[0]
    turned = [query_ref[h].T for h in range(heads)]
    for j in range(here + rows_ref.shape[0]):
        at = slice(j * span_rows, (j + 1) * span_rows)
        rows = jnp.concatenate([turned[h][at] for h in range(heads)], axis=0)
        if j >= here:
            rows_ref[j - here] = rows
            continue

        def store(h, part):
            out_ref[at, h * value : (h + 1) * value] = part

        length = lengths_ref[rank_ref[0] * (here + rows_ref.shape[0]) + j]
        attend_one(rows, length, prefix_ref[j], NN, span_ref[j], uv_ref, latent, store)


def moved_kernel(rank_ref, lengths_ref, destination_ref, rows_ref, prefix_ref, span_ref, uv_ref, out_ref):
    heads, latent, value = uv_ref.shape
    here, _, width = rows_ref.shape
    span_rows = span_ref.shape[1]
    for j in range(here):
        at = slice(j * span_rows, (j + 1) * span_rows)

        def store(h, part):
            out_ref[at, h * value : (h + 1) * value] = part

        ranks = destination_ref.shape[1]
        requests = lengths_ref.shape[0] // ranks
        source = jnp.int32(0)
        for s in range(ranks):
            source = jnp.where(destination_ref[j, s] == rank_ref[0], jnp.int32(s), source)
        length = lengths_ref[source * requests + requests - here + j]
        prefix = prefix_ref[:, j].reshape(-1, width)
        attend_one(rows_ref[j], length, prefix, NT, span_ref[j], uv_ref, latent, store)


def attend_call(kernel, operands, specs, shapes):
    flops = 2 * 2 * 128 * (288 * (576 + 512) + 512 * 128)
    outs = [jax.ShapeDtypeStruct(shape, bf16) for shape in shapes]
    return pl.pallas_call(
        kernel,
        out_shape=outs,
        in_specs=[pl.BlockSpec(memory_space=pltpu.SMEM)] * 3 + specs,
        out_specs=[whole(shape) for shape in shapes],
        grid=(1,),
        compiler_params=params(),
        cost_estimate=cost(flops, 2 << 20),
    )(*operands)


def whole(shape, block=0):
    return pl.BlockSpec(tuple(shape), lambda i: (block,) + (0,) * (len(shape) - 1))


def share_kernel(values_ref, weight_ref, out_ref, turned):
    @pl.when(pl.program_id(0) == 0)
    def _():
        turned[...] = values_ref[...].T

    blocks, half, depth = weight_ref.shape
    weight = weight_ref[...].reshape(blocks * half, depth)
    product = jnp.dot(weight, turned[...], preferred_element_type=f32).astype(bf16)
    out_ref[...] = product.reshape(out_ref.shape)


def project(values, weights, layers):
    rows, depth = values.shape
    blocks, half, _ = weights.shape
    each = blocks // layers
    steps = 2
    return pl.pallas_call(
        share_kernel,
        out_shape=jax.ShapeDtypeStruct((layers, each * half, rows), bf16),
        grid=(steps,),
        in_specs=[
            pl.BlockSpec((rows, depth), lambda i: (0, 0)),
            pl.BlockSpec((blocks // steps, half, depth), lambda i: (i, 0, 0)),
        ],
        out_specs=pl.BlockSpec((layers // steps, each * half, rows), lambda i: (i, 0, 0)),
        scratch_shapes=[pltpu.VMEM((depth, rows), bf16)],
        compiler_params=params(),
        cost_estimate=cost(
            2 * rows * depth * blocks * half,
            2 * (rows * depth + blocks * half * depth + blocks * half * rows),
        ),
    )(values, weights)


def hidden_kernel(width, rows_ref, weight_ref, out_ref, total, squares):
    step = pl.program_id(0)
    block = rows_ref[...]
    product = jnp.dot(weight_ref[...], block, preferred_element_type=f32)
    widened = block.astype(f32)
    square = jnp.sum(widened * widened, axis=0, keepdims=True)

    @pl.when(step == 0)
    def _():
        total[...] = product
        squares[...] = square

    @pl.when(step > 0)
    def _():
        total[...] += product
        squares[...] += square

    @pl.when(step == pl.num_programs(0) - 1)
    def _():
        factor = lax.rsqrt(squares[...] / width + norm_eps)
        ff = out_ref.shape[1]
        gate = total[:ff] * factor
        up = total[ff:] * factor
        out_ref[...] = (gate / (1.0 + jnp.exp(-gate)) * up).T.astype(bf16)


def hidden_of(rows_in, weight_in):
    width, slots = rows_in.shape
    ff = weight_in.shape[0] // 2
    steps = 2
    return pl.pallas_call(
        functools.partial(hidden_kernel, float(width)),
        out_shape=jax.ShapeDtypeStruct((slots, ff), bf16),
        grid=(steps,),
        in_specs=[
            pl.BlockSpec((width // steps, slots), lambda i: (i, 0)),
            pl.BlockSpec((2 * ff, width // steps), lambda i: (0, i)),
        ],
        out_specs=pl.BlockSpec((slots, ff), lambda i: (0, 0)),
        scratch_shapes=[pltpu.VMEM((2 * ff, slots), f32), pltpu.VMEM((1, slots), f32)],
        compiler_params=params(),
        cost_estimate=cost(4 * width * slots * ff, 2 * width * (slots + 2 * ff)),
    )(rows_in, weight_in)


def dispatch_kernel(capacity, top_k, shares_ref, packed_ref, mixed_ref, out_ref):
    col = mixed_ref.shape[0]
    total = packed_ref[:col].astype(f32)
    total += jnp.sum(shares_ref[...].astype(f32), axis=0)
    mixed = total.astype(bf16)
    mixed_ref[...] = mixed
    notes = packed_ref[col:].astype(f32)
    slot = lax.broadcasted_iota(jnp.int32, (out_ref.shape[0], mixed.shape[1]), 0)
    hit = None
    for k in range(top_k):
        named = notes[k : k + 1] * capacity + notes[top_k + k : top_k + k + 1]
        same = slot == named.astype(jnp.int32)
        hit = same if hit is None else hit | same
    placer = jnp.where(hit, 1.0, 0.0).astype(bf16)
    out_ref[...] = lax.dot_general(placer, mixed, NT, preferred_element_type=f32).astype(bf16)


def dispatch(shares, packed, capacity, top_k, slots):
    col, rows = shares.shape[1:]
    return pl.pallas_call(
        functools.partial(dispatch_kernel, capacity, top_k),
        out_shape=[
            jax.ShapeDtypeStruct((col, rows), bf16),
            jax.ShapeDtypeStruct((slots, col), bf16),
        ],
        grid=(1,),
        in_specs=[whole(shares.shape), whole(packed.shape)],
        out_specs=[whole((col, rows)), whole((slots, col))],
        compiler_params=params(),
        cost_estimate=cost(2 * slots * col * rows, 2 * (9 * col * rows + slots * col)),
    )(shares, packed)


def slices_kernel(layer_ref, in_ref, *refs):
    outs, (held, in_sems, out_sems) = refs[:-3], refs[-3:]
    count, rows, width = held.shape
    loads, stores = [], []
    for hops in range(count):
        at = pl.multiple_of(lax.rem(layer_ref[0] + hops, count) * width, 128)
        loads.append(
            pltpu.make_async_copy(in_ref.at[:, pl.ds(at, width)], held.at[hops], in_sems.at[hops])
        )
        stores.append(pltpu.make_async_copy(held.at[hops], outs[hops], out_sems.at[hops]))
    half = rows // 2
    stores[count // 2] = pltpu.make_async_copy(
        held.at[count // 2, pl.ds(0, half)], outs[count // 2], out_sems.at[count // 2]
    )
    stores.append(
        pltpu.make_async_copy(
            held.at[count // 2, pl.ds(half, half)], outs[count], out_sems.at[count]
        )
    )
    for load in loads:
        load.start()
    for hops, load in enumerate(loads):
        load.wait()
        stores[hops].start()
        if hops == count // 2:
            stores[count].start()
    for store in stores:
        store.wait()


def slices_of(layer, array, count):
    rows, columns = array.shape
    width = columns // count
    shapes = [(rows, width)] * (count + 1)
    shapes[count // 2] = shapes[count] = (rows // 2, width)
    return pl.pallas_call(
        slices_kernel,
        out_shape=[jax.ShapeDtypeStruct(shape, array.dtype) for shape in shapes],
        in_specs=[
            pl.BlockSpec(memory_space=pltpu.SMEM),
            pl.BlockSpec(memory_space=pl.ANY),
        ],
        out_specs=[pl.BlockSpec(memory_space=pl.ANY)] * (count + 1),
        scratch_shapes=[
            pltpu.VMEM((count, rows, width), array.dtype),
            pltpu.SemaphoreType.DMA((count,)),
            pltpu.SemaphoreType.DMA((count + 1,)),
        ],
        compiler_params=params(),
        cost_estimate=cost(0, 4 * rows * columns),
    )(layer, array)


def down_kernel(mine_ref, other_ref, mine_weight_ref, other_weight_ref, out_ref):
    depth = mine_ref.shape[1]
    total = jnp.dot(
        mine_ref[...], mine_weight_ref[...].reshape(depth, -1), preferred_element_type=f32
    )
    total += jnp.dot(
        other_ref[...], other_weight_ref[...].reshape(depth, -1), preferred_element_type=f32
    )
    out_ref[...] = total.astype(bf16)


def down_project(*operands):
    shape = (operands[0].shape[0], operands[2].shape[2])
    return pl.pallas_call(
        down_kernel,
        out_shape=jax.ShapeDtypeStruct(shape, bf16),
        grid=(1,),
        in_specs=[whole(o.shape) for o in operands],
        out_specs=whole(shape),
        compiler_params=params(),
        cost_estimate=cost(4 * shape[0] * shape[1] * operands[0].shape[1], 5 << 20),
    )(*operands)


def combine_kernel(combiner_ref, rows_ref, mixed_ref, out_ref):
    total = jnp.dot(combiner_ref[...], rows_ref[...], preferred_element_type=f32)
    out_ref[...] = (total + mixed_ref[...].astype(f32).T).astype(bf16)


def combine(combiner, rows, mixed):
    shape = (combiner.shape[0], rows.shape[1])
    return pl.pallas_call(
        combine_kernel,
        out_shape=jax.ShapeDtypeStruct(shape, bf16),
        grid=(1,),
        in_specs=[whole(o.shape) for o in (combiner, rows, mixed)],
        out_specs=whole(shape),
        compiler_params=params(),
        cost_estimate=cost(2 * shape[0] * shape[1] * rows.shape[0], 1 << 20),
    )(combiner, rows, mixed)


def places_of(route_rows, experts):
    flat_routes = route_rows.reshape(-1)
    hits = (flat_routes[:, None] == jnp.arange(experts, dtype=jnp.int32)[None, :]).astype(jnp.int32)
    earlier = jnp.cumsum(hits, axis=0) - hits
    return jnp.sum(earlier * hits, axis=1).reshape(route_rows.shape)


def per_device(
    queries,
    cache,
    span_latent,
    prefix_len,
    destination,
    uv_weight,
    out_weight,
    residual,
    norm_gain,
    routes,
    route_weight,
    gate_weight,
    up_weight,
    down_weight,
):
    requests, prefix_rows, cached_width = cache.shape
    tok_rows = queries.shape[0]
    model_width = residual.shape[1]
    top_k = routes.shape[1]
    ff = gate_weight.shape[2]
    nz = lax.axis_size("ep")
    rank_count = lax.axis_size(DP)
    members = lax.axis_size(MEM)
    my_rank = lax.axis_index(DP)
    member = lax.axis_index(MEM)
    layer = lax.axis_index("ep")
    core = lax.axis_index("tp")
    col = model_width // members
    capacity = max(2, 3 * tok_rows * top_k // (2 * rank_count))

    def other_core(array):
        return lax.ppermute(array, "tp", [(0, 1), (1, 0)])

    def along(array, hops):
        return lax.ppermute(array, "ep", [(z, (z + hops) % nz) for z in range(nz)])

    ranks = jnp.arange(rank_count, dtype=jnp.int32)
    source_first = jnp.sum(ranks * (destination[0] == my_rank).astype(jnp.int32))
    source_second = jnp.sum(ranks * (destination[1] == my_rank).astype(jnp.int32))
    part = prefix_rows // members
    moving = lax.dynamic_slice_in_dim(cache[requests - 2 :], member * part, part, 1)
    arrived = lax.all_to_all(
        jnp.broadcast_to(moving[None], (rank_count,) + moving.shape), DP, 0, 0, tiled=True
    )
    turned_out = out_weight.T.reshape(2, col // 2, -1)
    out_mine = lax.dynamic_index_in_dim(turned_out, core, 0, keepdims=False)
    out_other = other_core(lax.dynamic_index_in_dim(turned_out, 1 - core, 0, keepdims=False))
    out_cols = lax.all_gather(jnp.concatenate([out_mine, out_other], axis=1), DP, axis=0)
    slices = slices_of(jnp.reshape(layer, (1,)), down_weight[0], nz)
    middle = nz // 2

    down = {0: slices[0], 1: along(slices[1], 1), nz - 1: along(slices[nz - 1], -1)}
    arrived, down = lax.optimization_barrier((arrived, down))
    chosen = jnp.stack(
        [
            lax.dynamic_index_in_dim(arrived[:, 0], source_first, 0, keepdims=False),
            lax.dynamic_index_in_dim(arrived[:, 1], source_second, 0, keepdims=False),
        ]
    )
    moved = lax.all_gather(chosen, MEM, axis=0)

    window, held = lax.optimization_barrier(
        ((slices[3], slices[nz - 3], slices[middle], slices[nz]), (cache, routes, moved))
    )
    cache, routes, moved = held
    window = (
        along(window[0], 3),
        along(window[1], -3),
        along(window[2], middle),
        along(window[3], -middle),
    )

    heads, latent = queries.shape[1], uv_weight.shape[1]
    value = uv_weight.shape[2]
    here = requests - 2
    span_rows = span_latent.shape[1]
    values_shape = (2 * span_rows, heads * value)
    turned = (queries.transpose(1, 2, 0), cache.transpose(0, 2, 1))
    spans = (2, span_rows, cached_width)
    scalars = (jnp.reshape(my_rank, (1,)).astype(jnp.int32), prefix_len, destination)
    values_own, query_rows = attend_call(
        own_kernel,
        (*scalars, *turned, span_latent, uv_weight),
        [
            whole(turned[0].shape),
            whole((here, cached_width, prefix_rows)),
            whole(spans),
            whole(uv_weight.shape),
        ],
        [values_shape, (2, heads * span_rows, cached_width)],
    )

    (values_moved,) = attend_call(
        moved_kernel,
        (*scalars, query_rows, moved, span_latent, uv_weight),
        [whole(query_rows.shape), whole(moved.shape), whole(spans, 1), whole(uv_weight.shape)],
        [values_shape],
    )
    values = jnp.concatenate([values_own, values_moved], axis=0)

    places = places_of(routes, rank_count)
    residual_t = lax.dynamic_slice_in_dim(residual, layer * 2 * col, 2 * col, 1).T
    residual_t = residual_t.reshape(2, 2, col // 2, tok_rows)
    residual_t = lax.dynamic_index_in_dim(residual_t, core, 1, keepdims=False)
    packed = jnp.concatenate(
        [
            residual_t.reshape(col, tok_rows),
            routes.T.astype(bf16),
            places.T.astype(bf16),
            jnp.zeros((16 - 2 * top_k, tok_rows), bf16),
        ],
        axis=0,
    )
    values = jnp.concatenate([values, other_core(values)], axis=1)
    out_cols, window, packed = lax.optimization_barrier((out_cols, window, packed))
    down[3], down[nz - 3] = window[:2]
    down[middle] = jnp.concatenate(window[2:], axis=0)
    shares = project(values, out_cols, nz)

    norm_gain, route_weight, shares = lax.optimization_barrier((norm_gain, route_weight, shares))
    slot_index = jnp.arange(rank_count * capacity, dtype=jnp.int32)
    slots = (routes * capacity + places).T
    matches = slots[:, :, None] == slot_index[None, None, :]
    combiner = jnp.sum(
        jnp.where(matches, route_weight.T[:, :, None], jnp.zeros((), route_weight.dtype)), axis=0
    )
    gain = norm_gain.astype(f32)[:, None]
    weight_in = jnp.concatenate([gate_weight[0], up_weight[0]], axis=1)
    weight_in = (weight_in.astype(f32) * gain).astype(bf16)
    weight_in = weight_in.reshape(nz, 2, 2, col // 2, 2 * ff).transpose(0, 2, 1, 3, 4)
    weight_in = weight_in.reshape(model_width, 2 * ff).T
    shares = lax.all_to_all(shares, "ep", 0, 0, tiled=True)
    shares, down, combiner, weight_in = lax.optimization_barrier(
        (shares, down, combiner, weight_in)
    )

    window, _ = lax.optimization_barrier(((slices[2], slices[nz - 2]), shares))
    window = (along(window[0], 2), along(window[1], -2))
    mixed, outgoing = dispatch(shares, packed, capacity, top_k, rank_count * capacity)
    outgoing = outgoing.reshape(rank_count, capacity, col)
    received = lax.all_to_all(outgoing, DP, 0, 0, tiled=True)
    received, window = lax.optimization_barrier((received, window))
    down[2], down[nz - 2] = window
    received = received.reshape(rank_count * capacity, col).T
    down, _ = lax.optimization_barrier((down, received))
    down_all = jnp.stack([down[h] for h in range(nz)])
    half = col // 2
    even = jnp.concatenate([down_all[..., :half], down_all[..., col : col + half]], axis=2)
    odd = jnp.concatenate([down_all[..., half:col], down_all[..., col + half :]], axis=2)
    down_mine = jnp.where(core == 0, even, odd)
    down_other = other_core(jnp.where(core == 0, odd, even))
    rows_in = lax.all_gather(received, MEM, axis=0)
    rows_in, down_mine, down_other = lax.optimization_barrier((rows_in, down_mine, down_other))
    hidden = hidden_of(rows_in.reshape(model_width, -1), weight_in)

    half = hidden.shape[0] // 2
    blocks = {0: hidden}
    up_way, down_way = hidden, hidden
    for hops in range(1, middle):
        up_way, down_way = along(up_way, 1), along(down_way, -1)
        blocks[hops], blocks[nz - hops] = up_way, down_way
    blocks[middle] = jnp.concatenate([along(up_way[:half], 1), along(down_way[half:], -1)], axis=0)
    hidden_all = jnp.concatenate([blocks[h] for h in range(nz)], axis=1)
    expert_out = down_project(hidden_all, other_core(hidden_all), down_mine, down_other)
    expert_out = expert_out.reshape(rank_count, capacity, col)

    returned = lax.all_to_all(expert_out, DP, 0, 0, tiled=True)
    total = combine(combiner, returned.reshape(rank_count * capacity, col), mixed)
    group = tok_rows // members
    total = lax.all_to_all(total.reshape(members, group, col), MEM, 0, 0, tiled=True)
    total = total.reshape(nz, 2, group, 2, col // 2).transpose(2, 0, 3, 1, 4)
    return total.reshape(group, model_width)


def solution(mesh):
    in_specs = (
        P(DP, MEM, None),
        P(DP, None, None),
        P(DP, None, None),
        P(),
        P(),
        P(MEM, None, None),
        P(MEM, DP),
        P(DP, None),
        P(),
        P(DP, None),
        P(DP, None),
        P(DP, None, MEM),
        P(DP, None, MEM),
        P(DP, MEM, None),
    )
    out_specs = P(DP + MEM, None)
    return jax.shard_map(
        per_device, mesh=mesh, in_specs=in_specs, out_specs=out_specs, check_vma=False
    )
```

```python
import functools

import jax
import jax.numpy as jnp
from jax import lax
from jax.experimental import pallas as pl
from jax.experimental.pallas import tpu as pltpu
from jax.sharding import PartitionSpec as P

score_scale = 192.0 ** (-0.5)
norm_eps = 1e-06
DP = ("dp",)
MEM = ("ep", "tp")
bf16 = jnp.bfloat16
f32 = jnp.float32
VMEM_LIMIT = 56 << 20
NN = (((1,), (0,)), ((), ()))
NT = (((1,), (1,)), ((), ()))


def params():
    return pltpu.CompilerParams(vmem_limit_bytes=VMEM_LIMIT)


def cost(flops, nbytes):
    return pl.CostEstimate(flops=flops, bytes_accessed=nbytes, transcendentals=0)


def attend_one(rows, length, prefix, prefix_dims, span, uv_ref, latent, store):
    total, span_rows = rows.shape[0], span.shape[0]
    keys_first = prefix_dims is NT
    cached = prefix[:, :latent] if keys_first else prefix[:latent]
    first = lax.dot_general(rows, prefix, prefix_dims, preferred_element_type=f32) * score_scale
    second = lax.dot_general(rows, span, NT, preferred_element_type=f32) * score_scale
    key = lax.broadcasted_iota(jnp.int32, first.shape, 1)
    first = jnp.where(key < length, first, -jnp.inf)
    token = lax.rem(lax.broadcasted_iota(jnp.int32, second.shape, 0), span_rows)
    late = lax.broadcasted_iota(jnp.int32, second.shape, 1)
    second = jnp.where(late <= token, second, -jnp.inf)
    highest = jnp.maximum(
        jnp.max(first, axis=1, keepdims=True), jnp.max(second, axis=1, keepdims=True)
    )
    first = jnp.exp(first - highest)
    second = jnp.exp(second - highest)
    norm = jnp.sum(first, axis=1, keepdims=True) + jnp.sum(second, axis=1, keepdims=True)
    first = (first / norm).astype(bf16)
    second = (second / norm).astype(bf16)
    out = lax.dot_general(first, cached, NN if keys_first else NT, preferred_element_type=f32)
    out += jnp.dot(second, span[:, :latent], preferred_element_type=f32)
    out = out.astype(bf16)
    for h in range(total // span_rows):
        part = jnp.dot(
            out[h * span_rows : (h + 1) * span_rows], uv_ref[h], preferred_element_type=f32
        )
        store(h, part.astype(bf16))


def own_kernel(rank_ref, lengths_ref, destination_ref, query_ref, prefix_ref, span_ref, uv_ref, out_ref, rows_ref):
    heads, latent, value = uv_ref.shape
    span_rows = span_ref.shape[1]
    here = prefix_ref.shape[0]
    turned = [query_ref[h].T for h in range(heads)]
    for j in range(here + rows_ref.shape[0]):
        at = slice(j * span_rows, (j + 1) * span_rows)
        rows = jnp.concatenate([turned[h][at] for h in range(heads)], axis=0)
        if j >= here:
            rows_ref[j - here] = rows
            continue

        def store(h, part):
            out_ref[at, h * value : (h + 1) * value] = part

        length = lengths_ref[rank_ref[0] * (here + rows_ref.shape[0]) + j]
        attend_one(rows, length, prefix_ref[j], NN, span_ref[j], uv_ref, latent, store)


def moved_kernel(rank_ref, lengths_ref, destination_ref, rows_ref, prefix_ref, span_ref, uv_ref, out_ref):
    heads, latent, value = uv_ref.shape
    here, _, width = rows_ref.shape
    span_rows = span_ref.shape[1]
    for j in range(here):
        at = slice(j * span_rows, (j + 1) * span_rows)

        def store(h, part):
            out_ref[at, h * value : (h + 1) * value] = part

        ranks = destination_ref.shape[1]
        requests = lengths_ref.shape[0] // ranks
        source = jnp.int32(0)
        for s in range(ranks):
            source = jnp.where(destination_ref[j, s] == rank_ref[0], jnp.int32(s), source)
        length = lengths_ref[source * requests + requests - here + j]
        prefix = prefix_ref[:, j].reshape(-1, width)
        attend_one(rows_ref[j], length, prefix, NT, span_ref[j], uv_ref, latent, store)


def attend_call(kernel, operands, specs, shapes):
    flops = 2 * 2 * 128 * (288 * (576 + 512) + 512 * 128)
    outs = [jax.ShapeDtypeStruct(shape, bf16) for shape in shapes]
    return pl.pallas_call(
        kernel,
        out_shape=outs,
        in_specs=[pl.BlockSpec(memory_space=pltpu.SMEM)] * 3 + specs,
        out_specs=[whole(shape) for shape in shapes],
        grid=(1,),
        compiler_params=params(),
        cost_estimate=cost(flops, 2 << 20),
    )(*operands)


def whole(shape, block=0):
    return pl.BlockSpec(tuple(shape), lambda i: (block,) + (0,) * (len(shape) - 1))


def share_kernel(values_ref, weight_ref, out_ref, turned):
    @pl.when(pl.program_id(0) == 0)
    def _():
        turned[...] = values_ref[...].T

    blocks, half, depth = weight_ref.shape
    weight = weight_ref[...].reshape(blocks * half, depth)
    product = jnp.dot(weight, turned[...], preferred_element_type=f32).astype(bf16)
    out_ref[...] = product.reshape(out_ref.shape)


def project(values, weights, layers):
    rows, depth = values.shape
    blocks, half, _ = weights.shape
    each = blocks // layers
    steps = 2
    return pl.pallas_call(
        share_kernel,
        out_shape=jax.ShapeDtypeStruct((layers, each * half, rows), bf16),
        grid=(steps,),
        in_specs=[
            pl.BlockSpec((rows, depth), lambda i: (0, 0)),
            pl.BlockSpec((blocks // steps, half, depth), lambda i: (i, 0, 0)),
        ],
        out_specs=pl.BlockSpec((layers // steps, each * half, rows), lambda i: (i, 0, 0)),
        scratch_shapes=[pltpu.VMEM((depth, rows), bf16)],
        compiler_params=params(),
        cost_estimate=cost(
            2 * rows * depth * blocks * half,
            2 * (rows * depth + blocks * half * depth + blocks * half * rows),
        ),
    )(values, weights)


def hidden_kernel(width, rows_ref, weight_ref, out_ref, total, squares):
    step = pl.program_id(0)
    block = rows_ref[...]
    product = jnp.dot(weight_ref[...], block, preferred_element_type=f32)
    widened = block.astype(f32)
    square = jnp.sum(widened * widened, axis=0, keepdims=True)

    @pl.when(step == 0)
    def _():
        total[...] = product
        squares[...] = square

    @pl.when(step > 0)
    def _():
        total[...] += product
        squares[...] += square

    @pl.when(step == pl.num_programs(0) - 1)
    def _():
        factor = lax.rsqrt(squares[...] / width + norm_eps)
        ff = out_ref.shape[1]
        gate = total[:ff] * factor
        up = total[ff:] * factor
        out_ref[...] = (gate / (1.0 + jnp.exp(-gate)) * up).T.astype(bf16)


def hidden_of(rows_in, weight_in):
    width, slots = rows_in.shape
    ff = weight_in.shape[0] // 2
    steps = 2
    return pl.pallas_call(
        functools.partial(hidden_kernel, float(width)),
        out_shape=jax.ShapeDtypeStruct((slots, ff), bf16),
        grid=(steps,),
        in_specs=[
            pl.BlockSpec((width // steps, slots), lambda i: (i, 0)),
            pl.BlockSpec((2 * ff, width // steps), lambda i: (0, i)),
        ],
        out_specs=pl.BlockSpec((slots, ff), lambda i: (0, 0)),
        scratch_shapes=[pltpu.VMEM((2 * ff, slots), f32), pltpu.VMEM((1, slots), f32)],
        compiler_params=params(),
        cost_estimate=cost(4 * width * slots * ff, 2 * width * (slots + 2 * ff)),
    )(rows_in, weight_in)


def dispatch_kernel(capacity, top_k, shares_ref, packed_ref, mixed_ref, out_ref):
    col = mixed_ref.shape[0]
    total = packed_ref[:col].astype(f32)
    total += jnp.sum(shares_ref[...].astype(f32), axis=0)
    mixed = total.astype(bf16)
    mixed_ref[...] = mixed
    notes = packed_ref[col:].astype(f32)
    slot = lax.broadcasted_iota(jnp.int32, (out_ref.shape[0], mixed.shape[1]), 0)
    hit = None
    for k in range(top_k):
        named = notes[k : k + 1] * capacity + notes[top_k + k : top_k + k + 1]
        same = slot == named.astype(jnp.int32)
        hit = same if hit is None else hit | same
    placer = jnp.where(hit, 1.0, 0.0).astype(bf16)
    out_ref[...] = lax.dot_general(placer, mixed, NT, preferred_element_type=f32).astype(bf16)


def dispatch(shares, packed, capacity, top_k, slots):
    col, rows = shares.shape[1:]
    return pl.pallas_call(
        functools.partial(dispatch_kernel, capacity, top_k),
        out_shape=[
            jax.ShapeDtypeStruct((col, rows), bf16),
            jax.ShapeDtypeStruct((slots, col), bf16),
        ],
        grid=(1,),
        in_specs=[whole(shares.shape), whole(packed.shape)],
        out_specs=[whole((col, rows)), whole((slots, col))],
        compiler_params=params(),
        cost_estimate=cost(2 * slots * col * rows, 2 * (9 * col * rows + slots * col)),
    )(shares, packed)


def slices_kernel(layer_ref, in_ref, *refs):
    outs, (held, in_sems, out_sems) = refs[:-3], refs[-3:]
    count, rows, width = held.shape
    loads, stores = [], []
    for hops in range(count):
        at = pl.multiple_of(lax.rem(layer_ref[0] + hops, count) * width, 128)
        loads.append(
            pltpu.make_async_copy(in_ref.at[:, pl.ds(at, width)], held.at[hops], in_sems.at[hops])
        )
        stores.append(pltpu.make_async_copy(held.at[hops], outs[hops], out_sems.at[hops]))
    half = rows // 2
    stores[count // 2] = pltpu.make_async_copy(
        held.at[count // 2, pl.ds(0, half)], outs[count // 2], out_sems.at[count // 2]
    )
    stores.append(
        pltpu.make_async_copy(
            held.at[count // 2, pl.ds(half, half)], outs[count], out_sems.at[count]
        )
    )
    for load in loads:
        load.start()
    for hops, load in enumerate(loads):
        load.wait()
        stores[hops].start()
        if hops == count // 2:
            stores[count].start()
    for store in stores:
        store.wait()


def slices_of(layer, array, count):
    rows, columns = array.shape
    width = columns // count
    shapes = [(rows, width)] * (count + 1)
    shapes[count // 2] = shapes[count] = (rows // 2, width)
    return pl.pallas_call(
        slices_kernel,
        out_shape=[jax.ShapeDtypeStruct(shape, array.dtype) for shape in shapes],
        in_specs=[
            pl.BlockSpec(memory_space=pltpu.SMEM),
            pl.BlockSpec(memory_space=pl.ANY),
        ],
        out_specs=[pl.BlockSpec(memory_space=pl.ANY)] * (count + 1),
        scratch_shapes=[
            pltpu.VMEM((count, rows, width), array.dtype),
            pltpu.SemaphoreType.DMA((count,)),
            pltpu.SemaphoreType.DMA((count + 1,)),
        ],
        compiler_params=params(),
        cost_estimate=cost(0, 4 * rows * columns),
    )(layer, array)


def down_kernel(mine_weight_ref, other_weight_ref, *refs):
    hidden_refs, out_ref = refs[:-1], refs[-1]
    total = None
    for weight_ref, refs_here in (
        (mine_weight_ref, hidden_refs[:2]),
        (other_weight_ref, hidden_refs[2:]),
    ):
        first = 0
        for hidden_ref in refs_here:
            depth = hidden_ref.shape[1]
            hops = depth // weight_ref.shape[1]
            weight = weight_ref[first : first + hops].reshape(depth, -1)
            product = jnp.dot(hidden_ref[...], weight, preferred_element_type=f32)
            total = product if total is None else total + product
            first += hops
    out_ref[...] = total.astype(bf16)


def down_project(*operands):
    shape = (operands[2].shape[0], operands[0].shape[2])
    depth = operands[0].shape[0] * operands[0].shape[1]
    return pl.pallas_call(
        down_kernel,
        out_shape=jax.ShapeDtypeStruct(shape, bf16),
        grid=(1,),
        in_specs=[whole(o.shape) for o in operands],
        out_specs=whole(shape),
        compiler_params=params(),
        cost_estimate=cost(4 * shape[0] * shape[1] * depth, 5 << 20),
    )(*operands)


def combine_kernel(combiner_ref, rows_ref, mixed_ref, out_ref):
    total = jnp.dot(combiner_ref[...], rows_ref[...], preferred_element_type=f32)
    out_ref[...] = (total + mixed_ref[...].astype(f32).T).astype(bf16)


def combine(combiner, rows, mixed):
    shape = (combiner.shape[0], rows.shape[1])
    return pl.pallas_call(
        combine_kernel,
        out_shape=jax.ShapeDtypeStruct(shape, bf16),
        grid=(1,),
        in_specs=[whole(o.shape) for o in (combiner, rows, mixed)],
        out_specs=whole(shape),
        compiler_params=params(),
        cost_estimate=cost(2 * shape[0] * shape[1] * rows.shape[0], 1 << 20),
    )(combiner, rows, mixed)


def places_of(route_rows, experts):
    flat_routes = route_rows.reshape(-1)
    hits = (flat_routes[:, None] == jnp.arange(experts, dtype=jnp.int32)[None, :]).astype(jnp.int32)
    earlier = jnp.cumsum(hits, axis=0) - hits
    return jnp.sum(earlier * hits, axis=1).reshape(route_rows.shape)


def per_device(
    queries,
    cache,
    span_latent,
    prefix_len,
    destination,
    uv_weight,
    out_weight,
    residual,
    norm_gain,
    routes,
    route_weight,
    gate_weight,
    up_weight,
    down_weight,
):
    requests, prefix_rows, cached_width = cache.shape
    tok_rows = queries.shape[0]
    model_width = residual.shape[1]
    top_k = routes.shape[1]
    ff = gate_weight.shape[2]
    nz = lax.axis_size("ep")
    rank_count = lax.axis_size(DP)
    members = lax.axis_size(MEM)
    my_rank = lax.axis_index(DP)
    member = lax.axis_index(MEM)
    layer = lax.axis_index("ep")
    core = lax.axis_index("tp")
    col = model_width // members
    capacity = max(2, 3 * tok_rows * top_k // (2 * rank_count))

    def other_core(array):
        return lax.ppermute(array, "tp", [(0, 1), (1, 0)])

    def along(array, hops):
        return lax.ppermute(array, "ep", [(z, (z + hops) % nz) for z in range(nz)])

    ranks = jnp.arange(rank_count, dtype=jnp.int32)
    source_first = jnp.sum(ranks * (destination[0] == my_rank).astype(jnp.int32))
    source_second = jnp.sum(ranks * (destination[1] == my_rank).astype(jnp.int32))
    part = prefix_rows // members
    moving = lax.dynamic_slice_in_dim(cache[requests - 2 :], member * part, part, 1)
    arrived = lax.all_to_all(
        jnp.broadcast_to(moving[None], (rank_count,) + moving.shape), DP, 0, 0, tiled=True
    )
    turned_out = out_weight.T.reshape(2, col // 2, -1)
    out_mine = lax.dynamic_index_in_dim(turned_out, core, 0, keepdims=False)
    out_other = other_core(lax.dynamic_index_in_dim(turned_out, 1 - core, 0, keepdims=False))
    out_cols = lax.all_gather(jnp.concatenate([out_mine, out_other], axis=1), DP, axis=0)
    slices = slices_of(jnp.reshape(layer, (1,)), down_weight[0], nz)
    middle = nz // 2

    down = {0: slices[0], 1: along(slices[1], 1), nz - 1: along(slices[nz - 1], -1)}
    arrived, down = lax.optimization_barrier((arrived, down))
    chosen = jnp.stack(
        [
            lax.dynamic_index_in_dim(arrived[:, 0], source_first, 0, keepdims=False),
            lax.dynamic_index_in_dim(arrived[:, 1], source_second, 0, keepdims=False),
        ]
    )
    moved = lax.all_gather(chosen, MEM, axis=0)

    window, held = lax.optimization_barrier(
        ((slices[3], slices[nz - 3], slices[middle], slices[nz]), (cache, routes, moved))
    )
    cache, routes, moved = held
    window = (
        along(window[0], 3),
        along(window[1], -3),
        along(window[2], middle),
        along(window[3], -middle),
    )

    heads, latent = queries.shape[1], uv_weight.shape[1]
    value = uv_weight.shape[2]
    here = requests - 2
    span_rows = span_latent.shape[1]
    values_shape = (2 * span_rows, heads * value)
    turned = (queries.transpose(1, 2, 0), cache.transpose(0, 2, 1))
    spans = (2, span_rows, cached_width)
    scalars = (jnp.reshape(my_rank, (1,)).astype(jnp.int32), prefix_len, destination)
    values_own, query_rows = attend_call(
        own_kernel,
        (*scalars, *turned, span_latent, uv_weight),
        [
            whole(turned[0].shape),
            whole((here, cached_width, prefix_rows)),
            whole(spans),
            whole(uv_weight.shape),
        ],
        [values_shape, (2, heads * span_rows, cached_width)],
    )

    (values_moved,) = attend_call(
        moved_kernel,
        (*scalars, query_rows, moved, span_latent, uv_weight),
        [whole(query_rows.shape), whole(moved.shape), whole(spans, 1), whole(uv_weight.shape)],
        [values_shape],
    )
    values = jnp.concatenate([values_own, values_moved], axis=0)

    places = places_of(routes, rank_count)
    residual_t = lax.dynamic_slice_in_dim(residual, layer * 2 * col, 2 * col, 1).T
    residual_t = residual_t.reshape(2, 2, col // 2, tok_rows)
    residual_t = lax.dynamic_index_in_dim(residual_t, core, 1, keepdims=False)
    packed = jnp.concatenate(
        [
            residual_t.reshape(col, tok_rows),
            routes.T.astype(bf16),
            places.T.astype(bf16),
            jnp.zeros((16 - 2 * top_k, tok_rows), bf16),
        ],
        axis=0,
    )
    values = jnp.concatenate([values, other_core(values)], axis=1)
    out_cols, window, packed = lax.optimization_barrier((out_cols, window, packed))
    down[3], down[nz - 3] = window[:2]
    down[middle] = jnp.concatenate(window[2:], axis=0)
    shares = project(values, out_cols, nz)

    norm_gain, route_weight, shares = lax.optimization_barrier((norm_gain, route_weight, shares))
    slot_index = jnp.arange(rank_count * capacity, dtype=jnp.int32)
    slots = (routes * capacity + places).T
    matches = slots[:, :, None] == slot_index[None, None, :]
    combiner = jnp.sum(
        jnp.where(matches, route_weight.T[:, :, None], jnp.zeros((), route_weight.dtype)), axis=0
    )
    gain = norm_gain.astype(f32)[:, None]
    weight_in = jnp.concatenate([gate_weight[0], up_weight[0]], axis=1)
    weight_in = (weight_in.astype(f32) * gain).astype(bf16)
    weight_in = weight_in.reshape(nz, 2, 2, col // 2, 2 * ff).transpose(0, 2, 1, 3, 4)
    weight_in = weight_in.reshape(model_width, 2 * ff).T
    shares = lax.all_to_all(shares, "ep", 0, 0, tiled=True)
    shares, down, combiner, weight_in = lax.optimization_barrier(
        (shares, down, combiner, weight_in)
    )

    window, _ = lax.optimization_barrier(((slices[2], slices[nz - 2]), shares))
    window = (along(window[0], 2), along(window[1], -2))
    mixed, outgoing = dispatch(shares, packed, capacity, top_k, rank_count * capacity)
    outgoing = outgoing.reshape(rank_count, capacity, col)
    received = lax.all_to_all(outgoing, DP, 0, 0, tiled=True)
    received, window = lax.optimization_barrier((received, window))
    down[2], down[nz - 2] = window
    received = received.reshape(rank_count * capacity, col).T
    down, _ = lax.optimization_barrier((down, received))
    early = [0, 1, nz - 1, 2, nz - 2]
    late = [h for h in range(nz) if h not in early]
    down_all = jnp.stack([down[h] for h in early + late])
    half = col // 2
    even = jnp.concatenate([down_all[..., :half], down_all[..., col : col + half]], axis=2)
    odd = jnp.concatenate([down_all[..., half:col], down_all[..., col + half :]], axis=2)
    down_mine = jnp.where(core == 0, even, odd)
    down_other = other_core(jnp.where(core == 0, odd, even))
    rows_in = lax.all_gather(received, MEM, axis=0)
    rows_in, down_mine, down_other = lax.optimization_barrier((rows_in, down_mine, down_other))
    hidden = hidden_of(rows_in.reshape(model_width, -1), weight_in)

    half = hidden.shape[0] // 2
    blocks = {0: hidden}
    up_way, down_way = hidden, hidden
    for hops in range(1, middle):
        up_way, down_way = along(up_way, 1), along(down_way, -1)
        blocks[hops], blocks[nz - hops] = up_way, down_way
    blocks[middle] = jnp.concatenate([along(up_way[:half], 1), along(down_way[half:], -1)], axis=0)
    hidden_early = jnp.concatenate([blocks[h] for h in early], axis=1)
    hidden_late = jnp.concatenate([blocks[h] for h in late], axis=1)
    expert_out = down_project(
        down_mine,
        down_other,
        hidden_early,
        hidden_late,
        other_core(hidden_early),
        other_core(hidden_late),
    )
    expert_out = expert_out.reshape(rank_count, capacity, col)

    returned = lax.all_to_all(expert_out, DP, 0, 0, tiled=True)
    total = combine(combiner, returned.reshape(rank_count * capacity, col), mixed)
    group = tok_rows // members
    total = lax.all_to_all(total.reshape(members, group, col), MEM, 0, 0, tiled=True)
    total = total.reshape(nz, 2, group, 2, col // 2).transpose(2, 0, 3, 1, 4)
    return total.reshape(group, model_width)


def solution(mesh):
    in_specs = (
        P(DP, MEM, None),
        P(DP, None, None),
        P(DP, None, None),
        P(),
        P(),
        P(MEM, None, None),
        P(MEM, DP),
        P(DP, None),
        P(),
        P(DP, None),
        P(DP, None),
        P(DP, None, MEM),
        P(DP, None, MEM),
        P(DP, MEM, None),
    )
    out_specs = P(DP + MEM, None)
    return jax.shard_map(
        per_device, mesh=mesh, in_specs=in_specs, out_specs=out_specs, check_vma=False
    )
```

```python
import functools

import jax
import jax.numpy as jnp
from jax import lax
from jax.experimental import pallas as pl
from jax.experimental.pallas import tpu as pltpu
from jax.sharding import PartitionSpec as P

score_scale = 192.0 ** (-0.5)
norm_eps = 1e-06
DP = ("dp",)
MEM = ("ep", "tp")
bf16 = jnp.bfloat16
f32 = jnp.float32
VMEM_LIMIT = 56 << 20
NN = (((1,), (0,)), ((), ()))
NT = (((1,), (1,)), ((), ()))


def params():
    return pltpu.CompilerParams(vmem_limit_bytes=VMEM_LIMIT)


def cost(flops, nbytes):
    return pl.CostEstimate(flops=flops, bytes_accessed=nbytes, transcendentals=0)


def attend_one(rows, length, prefix, prefix_dims, span, uv_ref, latent, store):
    total, span_rows = rows.shape[0], span.shape[0]
    keys_first = prefix_dims is NT
    cached = prefix[:, :latent] if keys_first else prefix[:latent]
    first = lax.dot_general(rows, prefix, prefix_dims, preferred_element_type=f32) * score_scale
    second = lax.dot_general(rows, span, NT, preferred_element_type=f32) * score_scale
    key = lax.broadcasted_iota(jnp.int32, first.shape, 1)
    first = jnp.where(key < length, first, -jnp.inf)
    token = lax.rem(lax.broadcasted_iota(jnp.int32, second.shape, 0), span_rows)
    late = lax.broadcasted_iota(jnp.int32, second.shape, 1)
    second = jnp.where(late <= token, second, -jnp.inf)
    highest = jnp.maximum(
        jnp.max(first, axis=1, keepdims=True), jnp.max(second, axis=1, keepdims=True)
    )
    first = jnp.exp(first - highest)
    second = jnp.exp(second - highest)
    norm = jnp.sum(first, axis=1, keepdims=True) + jnp.sum(second, axis=1, keepdims=True)
    first = (first / norm).astype(bf16)
    second = (second / norm).astype(bf16)
    out = lax.dot_general(first, cached, NN if keys_first else NT, preferred_element_type=f32)
    out += jnp.dot(second, span[:, :latent], preferred_element_type=f32)
    out = out.astype(bf16)
    for h in range(total // span_rows):
        part = jnp.dot(
            out[h * span_rows : (h + 1) * span_rows], uv_ref[h], preferred_element_type=f32
        )
        store(h, part.astype(bf16))


def own_kernel(rank_ref, lengths_ref, destination_ref, query_ref, prefix_ref, span_ref, uv_ref, out_ref, rows_ref):
    heads, latent, value = uv_ref.shape
    span_rows = span_ref.shape[1]
    here = prefix_ref.shape[0]
    turned = [query_ref[h].T for h in range(heads)]
    for j in range(here + rows_ref.shape[0]):
        at = slice(j * span_rows, (j + 1) * span_rows)
        rows = jnp.concatenate([turned[h][at] for h in range(heads)], axis=0)
        if j >= here:
            rows_ref[j - here] = rows
            continue

        def store(h, part):
            out_ref[at, h * value : (h + 1) * value] = part

        length = lengths_ref[rank_ref[0] * (here + rows_ref.shape[0]) + j]
        attend_one(rows, length, prefix_ref[j], NN, span_ref[j], uv_ref, latent, store)


def moved_kernel(rank_ref, lengths_ref, destination_ref, rows_ref, prefix_ref, span_ref, uv_ref, out_ref):
    heads, latent, value = uv_ref.shape
    here, _, width = rows_ref.shape
    span_rows = span_ref.shape[1]
    for j in range(here):
        at = slice(j * span_rows, (j + 1) * span_rows)

        def store(h, part):
            out_ref[at, h * value : (h + 1) * value] = part

        ranks = destination_ref.shape[1]
        requests = lengths_ref.shape[0] // ranks
        source = jnp.int32(0)
        for s in range(ranks):
            source = jnp.where(destination_ref[j, s] == rank_ref[0], jnp.int32(s), source)
        length = lengths_ref[source * requests + requests - here + j]
        prefix = prefix_ref[:, j].reshape(-1, width)
        attend_one(rows_ref[j], length, prefix, NT, span_ref[j], uv_ref, latent, store)


def attend_call(kernel, operands, specs, shapes):
    flops = 2 * 2 * 128 * (288 * (576 + 512) + 512 * 128)
    outs = [jax.ShapeDtypeStruct(shape, bf16) for shape in shapes]
    return pl.pallas_call(
        kernel,
        out_shape=outs,
        in_specs=[pl.BlockSpec(memory_space=pltpu.SMEM)] * 3 + specs,
        out_specs=[whole(shape) for shape in shapes],
        grid=(1,),
        compiler_params=params(),
        cost_estimate=cost(flops, 2 << 20),
    )(*operands)


def whole(shape, block=0):
    return pl.BlockSpec(tuple(shape), lambda i: (block,) + (0,) * (len(shape) - 1))


def share_kernel(values_ref, weight_ref, out_ref, turned):
    @pl.when(pl.program_id(0) == 0)
    def _():
        turned[...] = values_ref[...].T

    blocks, half, depth = weight_ref.shape
    weight = weight_ref[...].reshape(blocks * half, depth)
    product = jnp.dot(weight, turned[...], preferred_element_type=f32).astype(bf16)
    out_ref[...] = product.reshape(out_ref.shape)


def project(values, weights, layers):
    rows, depth = values.shape
    blocks, half, _ = weights.shape
    each = blocks // layers
    steps = 2
    return pl.pallas_call(
        share_kernel,
        out_shape=jax.ShapeDtypeStruct((layers, each * half, rows), bf16),
        grid=(steps,),
        in_specs=[
            pl.BlockSpec((rows, depth), lambda i: (0, 0)),
            pl.BlockSpec((blocks // steps, half, depth), lambda i: (i, 0, 0)),
        ],
        out_specs=pl.BlockSpec((layers // steps, each * half, rows), lambda i: (i, 0, 0)),
        scratch_shapes=[pltpu.VMEM((depth, rows), bf16)],
        compiler_params=params(),
        cost_estimate=cost(
            2 * rows * depth * blocks * half,
            2 * (rows * depth + blocks * half * depth + blocks * half * rows),
        ),
    )(values, weights)


def hidden_kernel(width, rows_ref, weight_ref, out_ref, total, squares):
    step = pl.program_id(0)
    block = rows_ref[...]
    product = jnp.dot(weight_ref[...], block, preferred_element_type=f32)
    widened = block.astype(f32)
    square = jnp.sum(widened * widened, axis=0, keepdims=True)

    @pl.when(step == 0)
    def _():
        total[...] = product
        squares[...] = square

    @pl.when(step > 0)
    def _():
        total[...] += product
        squares[...] += square

    @pl.when(step == pl.num_programs(0) - 1)
    def _():
        factor = lax.rsqrt(squares[...] / width + norm_eps)
        ff = out_ref.shape[1]
        gate = total[:ff] * factor
        up = total[ff:] * factor
        out_ref[...] = (gate / (1.0 + jnp.exp(-gate)) * up).T.astype(bf16)


def hidden_of(rows_in, weight_in):
    width, slots = rows_in.shape
    ff = weight_in.shape[0] // 2
    steps = 2
    return pl.pallas_call(
        functools.partial(hidden_kernel, float(width)),
        out_shape=jax.ShapeDtypeStruct((slots, ff), bf16),
        grid=(steps,),
        in_specs=[
            pl.BlockSpec((width // steps, slots), lambda i: (i, 0)),
            pl.BlockSpec((2 * ff, width // steps), lambda i: (0, i)),
        ],
        out_specs=pl.BlockSpec((slots, ff), lambda i: (0, 0)),
        scratch_shapes=[pltpu.VMEM((2 * ff, slots), f32), pltpu.VMEM((1, slots), f32)],
        compiler_params=params(),
        cost_estimate=cost(4 * width * slots * ff, 2 * width * (slots + 2 * ff)),
    )(rows_in, weight_in)


def dispatch_kernel(capacity, top_k, shares_ref, packed_ref, mixed_ref, out_ref):
    col = mixed_ref.shape[0]
    total = packed_ref[:col].astype(f32)
    total += jnp.sum(shares_ref[...].astype(f32), axis=0)
    mixed = total.astype(bf16)
    mixed_ref[...] = mixed
    notes = packed_ref[col:].astype(f32)
    slot = lax.broadcasted_iota(jnp.int32, (out_ref.shape[0], mixed.shape[1]), 0)
    hit = None
    for k in range(top_k):
        named = notes[k : k + 1] * capacity + notes[top_k + k : top_k + k + 1]
        same = slot == named.astype(jnp.int32)
        hit = same if hit is None else hit | same
    placer = jnp.where(hit, 1.0, 0.0).astype(bf16)
    out_ref[...] = lax.dot_general(placer, mixed, NT, preferred_element_type=f32).astype(bf16)


def dispatch(shares, packed, capacity, top_k, slots):
    col, rows = shares.shape[1:]
    return pl.pallas_call(
        functools.partial(dispatch_kernel, capacity, top_k),
        out_shape=[
            jax.ShapeDtypeStruct((col, rows), bf16),
            jax.ShapeDtypeStruct((slots, col), bf16),
        ],
        grid=(1,),
        in_specs=[whole(shares.shape), whole(packed.shape)],
        out_specs=[whole((col, rows)), whole((slots, col))],
        compiler_params=params(),
        cost_estimate=cost(2 * slots * col * rows, 2 * (9 * col * rows + slots * col)),
    )(shares, packed)


def slices_kernel(layer_ref, in_ref, *refs):
    outs, (held, in_sems, out_sems) = refs[:-3], refs[-3:]
    count, rows, width = held.shape
    loads, stores = [], []
    for hops in range(count):
        at = pl.multiple_of(lax.rem(layer_ref[0] + hops, count) * width, 128)
        loads.append(
            pltpu.make_async_copy(in_ref.at[:, pl.ds(at, width)], held.at[hops], in_sems.at[hops])
        )
        stores.append(pltpu.make_async_copy(held.at[hops], outs[hops], out_sems.at[hops]))
    half = rows // 2
    stores[count // 2] = pltpu.make_async_copy(
        held.at[count // 2, pl.ds(0, half)], outs[count // 2], out_sems.at[count // 2]
    )
    stores.append(
        pltpu.make_async_copy(
            held.at[count // 2, pl.ds(half, half)], outs[count], out_sems.at[count]
        )
    )
    for load in loads:
        load.start()
    for hops, load in enumerate(loads):
        load.wait()
        stores[hops].start()
        if hops == count // 2:
            stores[count].start()
    for store in stores:
        store.wait()


def slices_of(layer, array, count):
    rows, columns = array.shape
    width = columns // count
    shapes = [(rows, width)] * (count + 1)
    shapes[count // 2] = shapes[count] = (rows // 2, width)
    return pl.pallas_call(
        slices_kernel,
        out_shape=[jax.ShapeDtypeStruct(shape, array.dtype) for shape in shapes],
        in_specs=[
            pl.BlockSpec(memory_space=pltpu.SMEM),
            pl.BlockSpec(memory_space=pl.ANY),
        ],
        out_specs=[pl.BlockSpec(memory_space=pl.ANY)] * (count + 1),
        scratch_shapes=[
            pltpu.VMEM((count, rows, width), array.dtype),
            pltpu.SemaphoreType.DMA((count,)),
            pltpu.SemaphoreType.DMA((count + 1,)),
        ],
        compiler_params=params(),
        cost_estimate=cost(0, 4 * rows * columns),
    )(layer, array)


def down_kernel(mine_weight_ref, other_weight_ref, *refs):
    hidden_refs, out_ref = refs[:-1], refs[-1]
    total = None
    for weight_ref, refs_here in (
        (mine_weight_ref, hidden_refs[:2]),
        (other_weight_ref, hidden_refs[2:]),
    ):
        first = 0
        for hidden_ref in refs_here:
            depth = hidden_ref.shape[1]
            hops = depth // weight_ref.shape[1]
            weight = weight_ref[first : first + hops].reshape(depth, -1)
            product = jnp.dot(hidden_ref[...], weight, preferred_element_type=f32)
            total = product if total is None else total + product
            first += hops
    out_ref[...] = total.astype(bf16)


def down_project(*operands):
    shape = (operands[2].shape[0], operands[0].shape[2])
    depth = operands[0].shape[0] * operands[0].shape[1]
    return pl.pallas_call(
        down_kernel,
        out_shape=jax.ShapeDtypeStruct(shape, bf16),
        grid=(1,),
        in_specs=[whole(o.shape) for o in operands],
        out_specs=whole(shape),
        compiler_params=params(),
        cost_estimate=cost(4 * shape[0] * shape[1] * depth, 5 << 20),
    )(*operands)


def combine_kernel(combiner_ref, rows_ref, mixed_ref, out_ref):
    total = jnp.dot(combiner_ref[...], rows_ref[...], preferred_element_type=f32)
    out_ref[...] = (total + mixed_ref[...].astype(f32).T).astype(bf16)


def combine(combiner, rows, mixed):
    shape = (combiner.shape[0], rows.shape[1])
    return pl.pallas_call(
        combine_kernel,
        out_shape=jax.ShapeDtypeStruct(shape, bf16),
        grid=(1,),
        in_specs=[whole(o.shape) for o in (combiner, rows, mixed)],
        out_specs=whole(shape),
        compiler_params=params(),
        cost_estimate=cost(2 * shape[0] * shape[1] * rows.shape[0], 1 << 20),
    )(combiner, rows, mixed)


def places_of(route_rows, experts):
    flat_routes = route_rows.reshape(-1)
    hits = (flat_routes[:, None] == jnp.arange(experts, dtype=jnp.int32)[None, :]).astype(jnp.int32)
    earlier = jnp.cumsum(hits, axis=0) - hits
    return jnp.sum(earlier * hits, axis=1).reshape(route_rows.shape)


def per_device(
    queries,
    cache,
    span_latent,
    prefix_len,
    destination,
    uv_weight,
    out_weight,
    residual,
    norm_gain,
    routes,
    route_weight,
    gate_weight,
    up_weight,
    down_weight,
):
    requests, prefix_rows, cached_width = cache.shape
    tok_rows = queries.shape[0]
    model_width = residual.shape[1]
    top_k = routes.shape[1]
    ff = gate_weight.shape[2]
    nz = lax.axis_size("ep")
    rank_count = lax.axis_size(DP)
    members = lax.axis_size(MEM)
    my_rank = lax.axis_index(DP)
    member = lax.axis_index(MEM)
    layer = lax.axis_index("ep")
    core = lax.axis_index("tp")
    col = model_width // members
    capacity = max(2, 3 * tok_rows * top_k // (2 * rank_count))

    def other_core(array):
        return lax.ppermute(array, "tp", [(0, 1), (1, 0)])

    def along(array, hops):
        return lax.ppermute(array, "ep", [(z, (z + hops) % nz) for z in range(nz)])

    ranks = jnp.arange(rank_count, dtype=jnp.int32)
    source_first = jnp.sum(ranks * (destination[0] == my_rank).astype(jnp.int32))
    source_second = jnp.sum(ranks * (destination[1] == my_rank).astype(jnp.int32))
    part = prefix_rows // members
    moving = lax.dynamic_slice_in_dim(cache[requests - 2 :], member * part, part, 1)
    arrived = lax.all_to_all(
        jnp.broadcast_to(moving[None], (rank_count,) + moving.shape), DP, 0, 0, tiled=True
    )
    turned_out = out_weight.T.reshape(2, col // 2, -1)
    out_mine = lax.dynamic_index_in_dim(turned_out, core, 0, keepdims=False)
    out_other = other_core(lax.dynamic_index_in_dim(turned_out, 1 - core, 0, keepdims=False))
    out_cols = lax.all_gather(jnp.concatenate([out_mine, out_other], axis=1), DP, axis=0)
    slices = slices_of(jnp.reshape(layer, (1,)), down_weight[0], nz)
    middle = nz // 2

    down = {0: slices[0], 1: along(slices[1], 1), nz - 1: along(slices[nz - 1], -1)}
    arrived, down = lax.optimization_barrier((arrived, down))
    chosen = jnp.stack(
        [
            lax.dynamic_index_in_dim(arrived[:, 0], source_first, 0, keepdims=False),
            lax.dynamic_index_in_dim(arrived[:, 1], source_second, 0, keepdims=False),
        ]
    )
    moved = lax.all_gather(chosen, MEM, axis=0)

    window, held = lax.optimization_barrier(
        ((slices[3], slices[nz - 3], slices[middle], slices[nz]), (routes, moved))
    )
    routes, moved = held
    window = (
        along(window[0], 3),
        along(window[1], -3),
        along(window[2], middle),
        along(window[3], -middle),
    )

    heads, latent = queries.shape[1], uv_weight.shape[1]
    value = uv_weight.shape[2]
    here = requests - 2
    span_rows = span_latent.shape[1]
    values_shape = (2 * span_rows, heads * value)
    turned = (queries.transpose(1, 2, 0), cache.transpose(0, 2, 1))
    spans = (2, span_rows, cached_width)
    scalars = (jnp.reshape(my_rank, (1,)).astype(jnp.int32), prefix_len, destination)
    values_own, query_rows = attend_call(
        own_kernel,
        (*scalars, *turned, span_latent, uv_weight),
        [
            whole(turned[0].shape),
            whole((here, cached_width, prefix_rows)),
            whole(spans),
            whole(uv_weight.shape),
        ],
        [values_shape, (2, heads * span_rows, cached_width)],
    )

    (values_moved,) = attend_call(
        moved_kernel,
        (*scalars, query_rows, moved, span_latent, uv_weight),
        [whole(query_rows.shape), whole(moved.shape), whole(spans, 1), whole(uv_weight.shape)],
        [values_shape],
    )
    values = jnp.concatenate([values_own, values_moved], axis=0)

    places = places_of(routes, rank_count)
    residual_t = lax.dynamic_slice_in_dim(residual, layer * 2 * col, 2 * col, 1).T
    residual_t = residual_t.reshape(2, 2, col // 2, tok_rows)
    residual_t = lax.dynamic_index_in_dim(residual_t, core, 1, keepdims=False)
    packed = jnp.concatenate(
        [
            residual_t.reshape(col, tok_rows),
            routes.T.astype(bf16),
            places.T.astype(bf16),
            jnp.zeros((16 - 2 * top_k, tok_rows), bf16),
        ],
        axis=0,
    )
    values = jnp.concatenate([values, other_core(values)], axis=1)
    out_cols, window, packed = lax.optimization_barrier((out_cols, window, packed))
    down[3], down[nz - 3] = window[:2]
    down[middle] = jnp.concatenate(window[2:], axis=0)
    shares = project(values, out_cols, nz)

    norm_gain, route_weight, shares = lax.optimization_barrier((norm_gain, route_weight, shares))
    slot_index = jnp.arange(rank_count * capacity, dtype=jnp.int32)
    slots = (routes * capacity + places).T
    matches = slots[:, :, None] == slot_index[None, None, :]
    combiner = jnp.sum(
        jnp.where(matches, route_weight.T[:, :, None], jnp.zeros((), route_weight.dtype)), axis=0
    )
    gain = norm_gain.astype(f32)[:, None]
    weight_in = jnp.concatenate([gate_weight[0], up_weight[0]], axis=1)
    weight_in = (weight_in.astype(f32) * gain).astype(bf16)
    weight_in = weight_in.reshape(nz, 2, 2, col // 2, 2 * ff).transpose(0, 2, 1, 3, 4)
    weight_in = weight_in.reshape(model_width, 2 * ff).T
    shares = lax.all_to_all(shares, "ep", 0, 0, tiled=True)
    shares, down, combiner, weight_in = lax.optimization_barrier(
        (shares, down, combiner, weight_in)
    )

    window, _ = lax.optimization_barrier(((slices[2], slices[nz - 2]), shares))
    window = (along(window[0], 2), along(window[1], -2))
    mixed, outgoing = dispatch(shares, packed, capacity, top_k, rank_count * capacity)
    outgoing = outgoing.reshape(rank_count, capacity, col)
    received = lax.all_to_all(outgoing, DP, 0, 0, tiled=True)
    received, window = lax.optimization_barrier((received, window))
    down[2], down[nz - 2] = window
    received = received.reshape(rank_count * capacity, col).T
    down, _ = lax.optimization_barrier((down, received))
    early = [0, 1, nz - 1, 2, nz - 2]
    late = [h for h in range(nz) if h not in early]
    down_all = jnp.stack([down[h] for h in early + late])
    half = col // 2
    even = jnp.concatenate([down_all[..., :half], down_all[..., col : col + half]], axis=2)
    odd = jnp.concatenate([down_all[..., half:col], down_all[..., col + half :]], axis=2)
    down_mine = jnp.where(core == 0, even, odd)
    down_other = other_core(jnp.where(core == 0, odd, even))
    rows_in = lax.all_gather(received, MEM, axis=0)
    rows_in, down_mine, down_other = lax.optimization_barrier((rows_in, down_mine, down_other))
    hidden = hidden_of(rows_in.reshape(model_width, -1), weight_in)

    half = hidden.shape[0] // 2
    blocks = {0: hidden}
    up_way, down_way = hidden, hidden
    for hops in range(1, middle):
        up_way, down_way = along(up_way, 1), along(down_way, -1)
        blocks[hops], blocks[nz - hops] = up_way, down_way
    blocks[middle] = jnp.concatenate([along(up_way[:half], 1), along(down_way[half:], -1)], axis=0)
    hidden_early = jnp.concatenate([blocks[h] for h in early], axis=1)
    hidden_late = jnp.concatenate([blocks[h] for h in late], axis=1)
    expert_out = down_project(
        down_mine,
        down_other,
        hidden_early,
        hidden_late,
        other_core(hidden_early),
        other_core(hidden_late),
    )
    expert_out = expert_out.reshape(rank_count, capacity, col)

    returned = lax.all_to_all(expert_out, DP, 0, 0, tiled=True)
    total = combine(combiner, returned.reshape(rank_count * capacity, col), mixed)
    group = tok_rows // members
    total = lax.all_to_all(total.reshape(members, group, col), MEM, 0, 0, tiled=True)
    total = total.reshape(nz, 2, group, 2, col // 2).transpose(2, 0, 3, 1, 4)
    return total.reshape(group, model_width)


def solution(mesh):
    in_specs = (
        P(DP, MEM, None),
        P(DP, None, None),
        P(DP, None, None),
        P(),
        P(),
        P(MEM, None, None),
        P(MEM, DP),
        P(DP, None),
        P(),
        P(DP, None),
        P(DP, None),
        P(DP, None, MEM),
        P(DP, None, MEM),
        P(DP, MEM, None),
    )
    out_specs = P(DP + MEM, None)
    return jax.shard_map(
        per_device, mesh=mesh, in_specs=in_specs, out_specs=out_specs, check_vma=False
    )
```
